32 devices in a mesh: rep: 8 (over y, x, core), zero: 4 (over z).
Axes of the slice: x: 2, y: 2, z: 4, core: 2. Of those that a mesh axis runs over, the one named last changes fastest.
Arguments:
- tokens: bfloat16 [8192, 1024], P(('rep', 'zero')), may hold values from -6 to 6
- cotangent: bfloat16 [8192, 1024], P(('rep', 'zero')), may hold values from -6 to 6
- seq_len: int32 [128], replicated, may hold values from 0 to 256, as said below
- seq_dev: int32 [128], replicated, may hold values from 0 to 31, as said below
- seq_off: int32 [128], replicated, may hold values from 0 to 256, as said below
- params: float32 [18355200], P(('rep', 'zero'))
- first_moment: float32 [18355200], P(('rep', 'zero'))
- second_moment: float32 [18355200], P(('rep', 'zero'))
Outputs:
- mixed: bfloat16 [8192, 1024], P(('rep', 'zero'))
- token_grad: bfloat16 [8192, 1024], P(('rep', 'zero'))
- param_grad: float32 [18355200], P(('rep', 'zero'))
- small_grad: float32 [5120], P(('rep', 'zero'))
- second_new: float32 [18355200], P(('rep', 'zero'))
- params_new: float32 [18355200], P(('rep', 'zero'))
The draws below stay inside these ranges and needn't reach their ends.
Inputs may be any that keep to these rules, and one draw needn't show every extreme that they name: `seq_len`: length of a record, 0 for an unused one. The records of one device lie one after another from slot 0 in the order of their seq_off and fill at most 256 slots; in every draw some device is full with a single record of length 256. `seq_dev`: device index in rep-major order; every device holds exactly 4 records. `seq_off`: A record's first slot on its device; records of a device do not intersect.
All inputs are finite; a program needn't handle non-finite values.
Results may differ from the reference program's by a relative error of at most 0.012.
Values may be sent and summed in bfloat16 or wider, within the bound.
No kernel may reach another device: no remote copies, remote signals or barrier semaphores. Data moves between devices by JAX's collectives and lax.ppermute only.
A program may use at most 320 MiB of HBM per device.

```python
import math
import jax
import jax.numpy as jnp
from jax import lax

D = 1024
FF = 4608
SLOTS = 256
SEQ_DEV = 4
STEP = 10
SHARDS = 32
TOKENS = 8192
NSEQ = 128
NPAR = 18355200


def deal(key):
    devices = NSEQ // SEQ_DEV
    key_total, key_full, key_cuts, key_order = jax.random.split(key, 4)
    totals = jax.random.randint(key_total, (devices,), 2 * SLOTS // 5, SLOTS + 1)
    chosen = jax.random.randint(key_full, (), 0, devices)
    filled = jnp.arange(devices) == chosen
    totals = jnp.where(filled, SLOTS, totals).astype(jnp.int32)
    cuts = jax.random.randint(key_cuts, (devices, SEQ_DEV - 1), 0, totals[:, None] + 1)
    cuts = jnp.where(filled[:, None], totals[:, None], cuts)
    cuts = jnp.sort(cuts, axis=1)
    bounds = jnp.concatenate([jnp.zeros((devices, 1), jnp.int32), cuts.astype(jnp.int32), totals[:, None]], axis=1)
    lengths = (bounds[:, 1:] - bounds[:, :-1]).reshape(-1)
    offsets = bounds[:, :-1].reshape(-1)
    owners = jnp.repeat(jnp.arange(devices, dtype=jnp.int32), SEQ_DEV)
    order = jax.random.permutation(key_order, NSEQ)
    seq_lengths = jnp.zeros((NSEQ,), jnp.int32).at[order].set(lengths)
    seq_owners = jnp.zeros((NSEQ,), jnp.int32).at[order].set(owners)
    seq_offsets = jnp.zeros((NSEQ,), jnp.int32).at[order].set(offsets)
    return (seq_lengths, seq_owners, seq_offsets)


def draw_seq_len(key, part):
    return deal(key)[0]


def draw_seq_dev(key, part):
    return deal(key)[1]


def draw_seq_off(key, part):
    return deal(key)[2]


def alternate(pieces):
    return jnp.concatenate([segment.reshape(SHARDS, -1) for segment in pieces], axis=1).reshape(-1)


def segment_sizes_drawn():
    return (3 * D * D, D * D, 2 * D * FF, FF * D, 5 * D)


def grad_scales():
    base = math.sqrt(0.7 * TOKENS)
    return (0.9 * base, 0.9 * base, 0.3 * base, 0.6 * base, 1.2 * base)


def draw_params(key, part):
    key = jax.random.fold_in(key, 11)
    keys = jax.random.split(key, 6)
    weight_in = jax.random.truncated_normal(keys[0], -4.0, 4.0, (3 * D * D,), jnp.float32) / math.sqrt(D)
    weight_out = jax.random.truncated_normal(keys[1], -4.0, 4.0, (D * D,), jnp.float32) / math.sqrt(D)
    weight_gateup = jax.random.truncated_normal(keys[2], -4.0, 4.0, (2 * D * FF,), jnp.float32) / math.sqrt(D)
    weight_down = jax.random.truncated_normal(keys[3], -4.0, 4.0, (FF * D,), jnp.float32) / math.sqrt(FF)
    gains = 1.0 + 0.3 * jax.random.uniform(keys[4], (2 * D,), jnp.float32, -1.0, 1.0)
    taps = 0.8 * jax.random.uniform(keys[5], (3 * D,), jnp.float32, -1.0, 1.0)
    small_params = jnp.concatenate([gains, taps])
    return alternate([weight_in, weight_out, weight_gateup, weight_down, small_params])


def draw_first_moment(key, part):
    key = jax.random.fold_in(key, 23)
    keys = jax.random.split(key, 5)
    pieces = []
    for number, extent in enumerate(segment_sizes_drawn()):
        scale = grad_scales()[number] / 9.0
        pieces.append(scale * jax.random.truncated_normal(keys[number], -4.0, 4.0, (extent,), jnp.float32))
    return alternate(pieces)


def draw_second_moment(key, part):
    key = jax.random.fold_in(key, 37)
    keys = jax.random.split(key, 5)
    pieces = []
    for number, extent in enumerate(segment_sizes_drawn()):
        scale = 2.0 * grad_scales()[number] ** 2 / 999.0
        factor = jnp.exp(jax.random.uniform(keys[number], (extent,), jnp.float32, math.log(0.5), math.log(2.0)))
        pieces.append(scale * factor)
    return alternate(pieces)


def with_spikes(result, stream_key, source, target, blocks, factor):
    owner, partner = [(jnp.arange(result.shape[dim]) // (result.shape[dim] // blocks)).reshape([-1 if axis == dim else 1 for axis in range(result.ndim)]) for dim in (source, target)]
    chosen = jax.random.permutation(stream_key, blocks)[partner]
    strong = (owner == chosen) | (owner == (partner + blocks // 2) % blocks)
    return jnp.where(strong, factor * result, result)


def block_levels(own_key, shape, shards, low, largest):
    loudness, own = 1.0, jax.random.fold_in(own_key, 6)
    for axis_at, blocks in shards:
        draws = jnp.exp(jax.random.uniform(jax.random.fold_in(own, axis_at), (blocks,), jnp.float32, low / len(shards), largest / len(shards)))
        loudness = loudness * jnp.repeat(draws, shape[axis_at] // blocks).reshape([-1 if axis == axis_at else 1 for axis in range(len(shape))])
    return loudness


def centred(key, dims, width, most, shards=(), held_as=jnp.bfloat16):
    array = width * jax.random.normal(key, dims, jnp.float32)
    if shards:
        array = array * block_levels(key, dims, shards, -0.22, 0.18)
    return jnp.clip(array, -most, most).astype(held_as)


def noise_with(own_key, dims, deviation, most, cuts, heavy, kind=jnp.bfloat16):
    values = deviation * jax.random.normal(own_key, dims, jnp.float32)
    if cuts:
        values = values * block_levels(own_key, dims, cuts, -0.22, 0.18)
    return jnp.clip(with_spikes(values, jax.random.fold_in(own_key, 3), *heavy), -most, most).astype(kind)


def setup_inputs(seed: int = 0) -> dict:
    key_of = jax.random.split(jax.random.key(seed), 9)
    tokens = noise_with(key_of[0], (TOKENS, D), 1.0, 6.0, ((0, 32),), (0, 1, 32, 2.75))
    cotangent = centred(key_of[1], (TOKENS, D), 1.0, 6.0, ((0, 32),))
    seq_len = draw_seq_len(jax.random.fold_in(key_of[8], 71), 0)
    seq_dev = draw_seq_dev(jax.random.fold_in(key_of[8], 71), 0)
    seq_off = draw_seq_off(jax.random.fold_in(key_of[8], 71), 0)
    params = draw_params(jax.random.fold_in(key_of[8], 71), 0)
    first_moment = draw_first_moment(jax.random.fold_in(key_of[8], 71), 0)
    second_moment = draw_second_moment(jax.random.fold_in(key_of[8], 71), 0)
    return dict(tokens=tokens, cotangent=cotangent, seq_len=seq_len, seq_dev=seq_dev, seq_off=seq_off, params=params, first_moment=first_moment, second_moment=second_moment)


@jax.custom_vjp
def low(v):
    return lax.optimization_barrier(v.astype(jnp.bfloat16)).astype(jnp.float32)

@jax.custom_vjp
def low_back(v):
    return v

def low_keep(v):
    return (low(v), None)

def low_pass(kept, grad):
    return (grad,)

def back_keep(v):
    return (v, None)

def back_low(kept, grad):
    return (low(grad),)
low.defvjp(low_keep, low_pass)
low_back.defvjp(back_keep, back_low)
norm_epsilon = 1e-05
first_decay = 0.9
second_decay = 0.999
moment_epsilon = 1e-08
weight_decay = 0.1
learn_rate = 0.06

def segment_sizes():
    return (3 * D * D, D * D, 2 * D * FF, FF * D, 5 * D)

def unpack(vector):
    matrix_view = vector.reshape(SHARDS, -1)
    pieces = []
    offset = 0
    for extent in segment_sizes():
        columns = extent // SHARDS
        pieces.append(matrix_view[:, offset:offset + columns].reshape(-1))
        offset = offset + columns
    return pieces

def pack(pieces):
    return jnp.concatenate([segment.reshape(SHARDS, -1) for segment in pieces], axis=1).reshape(-1)

def layout(starts, lengths, slot_count):
    nonempty = lengths > 0
    opening = jnp.where(nonempty, starts, slot_count).astype(jnp.int32)
    closing = jnp.where(nonempty, starts + lengths, slot_count).astype(jnp.int32)
    markers = jnp.full((slot_count,), -1, jnp.int32).at[opening].max(starts.astype(jnp.int32), mode='drop')
    latest = lax.cummax(markers, axis=0)
    position = jnp.arange(slot_count, dtype=jnp.int32) - latest
    boundary = jnp.zeros((slot_count,), jnp.int32).at[opening].add(1, mode='drop').at[closing].add(-1, mode='drop')
    occupied = jnp.cumsum(boundary) > 0
    return (position, occupied)

def rms_scale(values):
    return lax.rsqrt(lax.optimization_barrier(jnp.mean(values * values, axis=-1, keepdims=True)) + norm_epsilon)

def shift_down(values, steps):
    return jnp.pad(values, ((steps, 0), (0, 0)))[:values.shape[0]]

def matmul(left, right):
    return jnp.dot(left, right, precision=lax.Precision.HIGHEST, preferred_element_type=jnp.float32)

def forward(inputs, weights, position, occupied):
    weight_in = low(weights[0]).reshape(D, 3 * D)
    weight_out = low(weights[1]).reshape(D, D)
    weight_gateup = low(weights[2]).reshape(D, 2 * FF)
    weight_down = low(weights[3]).reshape(FF, D)
    small_params = low(weights[4]).reshape(5, D)
    keeper = occupied.astype(jnp.float32)[:, None]
    reach_one = (occupied & (position >= 1)).astype(jnp.float32)[:, None]
    reach_two = (occupied & (position >= 2)).astype(jnp.float32)[:, None]
    normed = low(inputs * rms_scale(inputs) * small_params[0])
    mixin = low_back(matmul(normed, weight_in))
    b_part = mixin[:, :D]
    c_part = mixin[:, D:2 * D]
    v_part = mixin[:, 2 * D:]
    product = b_part * v_part
    convolved = small_params[2] * product + small_params[3] * shift_down(product, 1) * reach_one + small_params[4] * shift_down(product, 2) * reach_two
    gated = low(c_part * convolved)
    branch = low_back(matmul(gated, weight_out))
    middle = inputs + keeper * branch
    normed_two = low(middle * rms_scale(middle) * small_params[1])
    gate_up = low_back(matmul(normed_two, weight_gateup))
    hidden = low(jax.nn.silu(gate_up[:, :FF]) * gate_up[:, FF:])
    feed_out = low_back(matmul(hidden, weight_down))
    return middle + keeper * feed_out

def reference(tokens, cotangent, seq_len, seq_dev, seq_off, params, first_moment, second_moment):
    position, occupied = layout(seq_dev * SLOTS + seq_off, seq_len, TOKENS)
    weights = unpack(params)
    inputs = tokens.astype(jnp.float32).reshape(SHARDS, SLOTS, D)
    backs = cotangent.astype(jnp.float32).reshape(SHARDS, SLOTS, D)

    def visit(running, item):
        block_in, block_back, block_pos, block_live = item

        def local_forward(values, *parts):
            return forward(values, parts, block_pos, block_live)
        outputs, pullback = jax.vjp(local_forward, block_in, *weights)
        grads = pullback(block_back)
        running = tuple((older + newer for older, newer in zip(running, grads[1:])))
        return (running, (outputs.astype(jnp.bfloat16), grads[0].astype(jnp.bfloat16)))
    initial = tuple((jnp.zeros_like(segment) for segment in weights))
    totals, (mixed, token_grad) = lax.scan(visit, initial, (inputs, backs, position.reshape(SHARDS, SLOTS), occupied.reshape(SHARDS, SLOTS)))
    param_grad = pack(list(totals))
    small_grad = totals[4]
    matrix_mask = (jnp.arange(NPAR // SHARDS) < (NPAR - 5 * D) // SHARDS).astype(jnp.float32)
    matrix_mask = jnp.tile(matrix_mask, SHARDS)
    moment = first_decay * first_moment + (1.0 - first_decay) * param_grad
    second_new = second_decay * second_moment + (1.0 - second_decay) * param_grad * param_grad
    moment_hat = moment / (1.0 - first_decay ** STEP)
    second_hat = second_new / (1.0 - second_decay ** STEP)
    params_new = params - learn_rate * (moment_hat / (jnp.sqrt(second_hat) + moment_epsilon) + weight_decay * matrix_mask * params)
    return (mixed.reshape(TOKENS, D), token_grad.reshape(TOKENS, D), param_grad, small_grad, second_new, params_new)
```

```python
import jax
import jax.numpy as jnp
from jax import lax
from jax.sharding import PartitionSpec as P

D = 1024
FF = 4608
STEP = 10
AXES = ("rep", "zero")
TEAM = 4
DQ = D // TEAM
FQ = FF // TEAM
SMALL = 5
PAD = 128

norm_epsilon = 1e-05
first_decay = 0.9
second_decay = 0.999
moment_epsilon = 1e-08
weight_decay = 0.1
learn_rate = 0.06


def rms_scale(values):
    return lax.rsqrt(jnp.mean(values * values, axis=-1, keepdims=True) + norm_epsilon)


def shift_down(values, steps):
    return jnp.pad(values, ((steps, 0), (0, 0)))[: values.shape[0]]


def shift_up(values, steps):
    return jnp.pad(values, ((0, steps), (0, 0)))[steps:]


def matmul(left, right):
    return jnp.dot(left, right, preferred_element_type=jnp.float32)


def over_rows(left, right):
    return lax.dot_general(
        left, right, (((0,), (0,)), ((), ())), preferred_element_type=jnp.float32
    )


def against(left, right):
    return lax.dot_general(
        left, right, (((1,), (1,)), ((), ())), preferred_element_type=jnp.float32
    )


def slot_masks(seq_len, seq_dev, seq_off, owners, slots):
    index = jnp.arange(slots, dtype=jnp.int32)[None, :, None]
    mine = seq_dev[None, None, :] == owners[:, None, None]
    start = seq_off[None, None, :]
    covers = mine & (index >= start) & (index < start + seq_len[None, None, :])
    live = jnp.any(covers, axis=-1)
    opening = jnp.sum(jnp.where(covers, start, 0), axis=-1)
    position = index[:, :, 0] - opening
    column = lambda flags: flags.astype(jnp.float32).reshape(-1, 1)
    return column(live), column(live & (position >= 1)), column(live & (position >= 2))


def local(tokens, cotangent, seq_len, seq_dev, seq_off, params, first_moment, second_moment):
    shards = lax.axis_size(AXES)
    line = lax.axis_size("zero")
    device = lax.axis_index(AXES)
    ring = shards // TEAM
    quarter = device // ring
    slots = tokens.shape[0]
    rings = [[q * ring + w for w in range(ring)] for q in range(TEAM)]
    peers = [quarter ^ j for j in range(TEAM)]

    def send(value, flip):
        return lax.ppermute(value, AXES, [(k, k ^ flip) for k in range(shards)])

    def spread(value):
        return [value] + [send(value, j * ring) for j in range(1, TEAM)]

    def swap(blocks):
        return [blocks[0]] + [send(blocks[j], j * ring) for j in range(1, TEAM)]

    def in_order(pieces):
        odd, high = quarter % 2 == 1, quarter // 2 == 1
        low = [jnp.where(odd, pieces[i ^ 1], pieces[i]) for i in range(TEAM)]
        return jnp.stack([jnp.where(high, low[i ^ 2], low[i]) for i in range(TEAM)])

    def take(table, index, axis):
        return lax.dynamic_index_in_dim(table, index, axis=axis, keepdims=False)

    def pick(table, axis):
        return [take(table, peer, axis) for peer in peers]

    def after(value, earlier):
        return lax.optimization_barrier((value, earlier))

    def ring_gather(value, axis):
        return lax.all_gather(value, AXES, axis=axis, tiled=True, axis_index_groups=rings)

    core_flips = [ring >> i for i in range(1, ring.bit_length()) if ring >> i >= line]
    line_flips = [1 << i for i in range(line.bit_length() - 1)]

    def fold(value, axis, flips):
        for flip in flips:
            shape = value.shape
            half = shape[axis] // 2
            cut, place = ((2, half), axis) if flip >= line else ((half, 2), axis + 1)
            value = value.reshape(shape[:axis] + cut + shape[axis + 1 :])
            bit = (device // flip) % 2
            other = send(take(value, 1 - bit, place), flip)
            value = take(value, bit, place).astype(jnp.float32) + other.astype(jnp.float32)
            value = value.astype(jnp.bfloat16)
        return value

    rows = D // shards
    sizes = (rows * 3 * D, rows * D, rows * 2 * FF, FF // shards * D, SMALL * rows)
    starts = [sum(sizes[:i]) for i in range(6)]
    share = [params[starts[i] : starts[i + 1]] for i in range(5)]
    low = [part.astype(jnp.bfloat16) for part in share]

    deep = FF // shards
    block_early = jnp.concatenate([low[3].reshape(deep, D), low[1].reshape(rows, D)], axis=0)
    ring_early = ring_gather(block_early, 0).reshape(ring, deep + rows, D)

    block_small = jnp.pad(low[4].reshape(rows, SMALL), ((0, 0), (0, PAD - SMALL)))
    block_in = pick(low[0].reshape(rows, 3, TEAM, DQ), 2)
    block_in = [jnp.concatenate([b.reshape(rows, 3 * DQ), block_small], axis=1) for b in block_in]
    block_in = swap(block_in)
    block_in, own_tokens = after(block_in, tokens)
    token_parts = spread(own_tokens)
    block_in, ring_early = after(in_order(block_in), ring_early)
    ring_in = ring_gather(block_in, 1)

    token_parts, block_gu = after(token_parts, low[2])
    block_gu = pick(block_gu.reshape(rows, 2, TEAM, FQ), 2)
    block_gu = in_order(swap([b.reshape(rows, 2 * FQ) for b in block_gu]))
    weight_gateup = ring_gather(block_gu, 1).reshape(D, 2 * FQ)
    token_parts, late_cotangent = after(token_parts, cotangent)
    cotangent_parts = spread(late_cotangent)
    weight_down = ring_early[:, :deep].reshape(FQ, D)
    weight_out = ring_early[:, deep:].reshape(DQ, D)
    cotangent_parts, weight_out = after(cotangent_parts, weight_out)
    weight_out = spread(weight_out)
    weight_in = ring_in[:, :, : 3 * DQ].reshape(D, 3 * DQ)
    small = ring_in[:, :, 3 * DQ : 3 * DQ + SMALL].astype(jnp.float32).reshape(SMALL, D)
    gain_one = small[0]
    gain_two = small[1]
    taps = lax.dynamic_slice(small, (2, quarter * DQ), (3, DQ))

    owners = jnp.stack([peer * ring + device % ring for peer in peers])
    live, reach_one, reach_two = slot_masks(seq_len, seq_dev, seq_off, owners, slots)
    keeper = live[:slots]

    inputs = jnp.concatenate(token_parts, axis=0).astype(jnp.float32)
    unit_one = inputs * rms_scale(inputs)
    normed = (unit_one * gain_one).astype(jnp.bfloat16)
    mixin = matmul(normed, weight_in)
    b_part = mixin[:, :DQ]
    c_part = mixin[:, DQ : 2 * DQ]
    v_part = mixin[:, 2 * DQ :]
    product = b_part * v_part
    lag_one = shift_down(product, 1) * reach_one
    lag_two = shift_down(product, 2) * reach_two
    convolved = taps[0] * product + taps[1] * lag_one + taps[2] * lag_two
    gated = (c_part * convolved).astype(jnp.bfloat16)
    gated = swap([gated[j * slots : (j + 1) * slots] for j in range(TEAM)])

    own = tokens.astype(jnp.float32)
    own_scale = rms_scale(own)
    own_unit = own * own_scale
    branch = sum(matmul(gated[j], weight_out[j]) for j in range(TEAM))
    middle = own + keeper * branch
    scale_two = rms_scale(middle)
    unit_two = middle * scale_two
    normed_two = (unit_two * gain_two).astype(jnp.bfloat16)
    normed_two = spread(normed_two)

    upstream = jnp.concatenate(cotangent_parts, axis=0).astype(jnp.float32)
    feed_back = (live * upstream).astype(jnp.bfloat16)
    gate_up = matmul(jnp.concatenate(normed_two, axis=0), weight_gateup)
    gate_part = gate_up[:, :FQ]
    up_part = gate_up[:, FQ:]
    sigma = jax.nn.sigmoid(gate_part)
    swish = gate_part * sigma
    hidden = (swish * up_part).astype(jnp.bfloat16)
    hidden_back = against(feed_back, weight_down)
    gate_back = hidden_back * up_part * (sigma + gate_part * sigma * (1.0 - sigma))
    up_back = hidden_back * swish
    gateup_back = jnp.concatenate([gate_back, up_back], axis=1).astype(jnp.bfloat16)

    spans = [slice(j * slots, (j + 1) * slots) for j in range(TEAM)]
    normed_two_back = against(gateup_back, weight_gateup).astype(jnp.bfloat16)
    normed_two_back = [normed_two_back[span] for span in spans]
    normed_two_back, hidden = after(normed_two_back, hidden)
    normed_two_back = swap(normed_two_back)

    grad_down = over_rows(hidden, feed_back).astype(jnp.bfloat16)
    grad_down = fold(grad_down.reshape(ring, deep, D), 0, core_flips)
    early, (normed_two, hidden) = after(normed_two_back[1:3], (normed_two, hidden))
    feed_out = matmul(hidden, weight_down).astype(jnp.bfloat16)
    grad_gate = over_rows(jnp.concatenate(normed_two, axis=0), gateup_back[:, :FQ]).astype(jnp.bfloat16)
    grad_gate = fold(grad_gate.reshape(TEAM, ring, rows, FQ), 1, core_flips)
    grad_down = fold(grad_down, 0, line_flips[:1])
    normed_two_back = [normed_two_back[0], early[0], early[1], normed_two_back[3]]
    normed_two_back, (grad_down, grad_gate, feed_out) = after(
        normed_two_back, (grad_down, grad_gate, feed_out)
    )
    grad_down = fold(grad_down, 0, line_flips[1:])
    grad_gate = fold(grad_gate, 1, line_flips[:1])
    normed_two_back = sum(part.astype(jnp.float32) for part in normed_two_back)

    grad_gain_two = jnp.sum(normed_two_back * unit_two, axis=0)
    unit_two_back = normed_two_back * gain_two
    own_back = cotangent.astype(jnp.float32)
    middle_back = own_back + scale_two * (
        unit_two_back - unit_two * jnp.mean(unit_two_back * unit_two, axis=-1, keepdims=True)
    )
    branch_back = (keeper * middle_back).astype(jnp.bfloat16)
    gated_back = [against(branch_back, weight_out[j]).astype(jnp.bfloat16) for j in range(TEAM)]
    gated_back = swap(gated_back)
    gated_back[1], (gated, branch_back, normed_two) = after(
        gated_back[1], (gated, branch_back, normed_two)
    )
    grad_up = over_rows(jnp.concatenate(normed_two, axis=0), gateup_back[:, FQ:]).astype(jnp.bfloat16)
    grad_out = [over_rows(gated[j], branch_back).astype(jnp.bfloat16) for j in range(TEAM)]
    grad_out = swap(grad_out)
    gated_back, (grad_down, grad_gate) = after(gated_back, (grad_down, grad_gate))
    gated_back = jnp.concatenate(gated_back, axis=0).astype(jnp.float32)
    grad_up = fold(grad_up.reshape(TEAM, ring, rows, FQ), 1, core_flips)
    grad_gate = fold(grad_gate, 1, line_flips[1:])

    conv_back = gated_back * c_part
    c_back = gated_back * convolved
    grad_taps = jnp.stack(
        [
            jnp.sum(conv_back * product, axis=0),
            jnp.sum(conv_back * lag_one, axis=0),
            jnp.sum(conv_back * lag_two, axis=0),
        ]
    )
    product_back = (
        taps[0] * conv_back
        + shift_up(taps[1] * conv_back * reach_one, 1)
        + shift_up(taps[2] * conv_back * reach_two, 2)
    )
    mixin_back = jnp.concatenate(
        [product_back * v_part, c_back, product_back * b_part], axis=1
    ).astype(jnp.bfloat16)
    normed_back = against(mixin_back, weight_in)
    grad_gain_one = jnp.sum(normed_back * unit_one, axis=0)
    normed_back = normed_back.astype(jnp.bfloat16)
    normed_back = [jnp.concatenate([normed_back[span], feed_out[span]], axis=0) for span in spans]
    normed_back, (grad_gate, grad_up) = after(normed_back, (grad_gate, grad_up))
    normed_back = swap(normed_back)
    grad_out = sum(part.astype(jnp.float32) for part in grad_out).astype(jnp.bfloat16)
    grad_up = fold(grad_up, 1, line_flips[:1])
    small_terms = lax.dynamic_update_slice(
        jnp.zeros((SMALL, D), jnp.float32), grad_taps, (2, quarter * DQ)
    )
    small_terms = small_terms.at[0].set(grad_gain_one).at[1].set(grad_gain_two)
    small_terms = jnp.pad(small_terms.reshape(D, SMALL), ((0, 0), (0, PAD - SMALL)))
    grad_tail = [
        over_rows(normed, mixin_back).astype(jnp.bfloat16).reshape(TEAM, ring, rows, 3 * DQ),
        small_terms.astype(jnp.bfloat16).reshape(TEAM, ring, rows, PAD),
        grad_out.reshape(ring, rows, TEAM, DQ).transpose(2, 0, 1, 3),
    ]
    grad_tail = jnp.concatenate(grad_tail, axis=3)
    grad_tail = fold(grad_tail, 1, core_flips)
    grad_up = fold(grad_up, 1, line_flips[1:])
    grad_tail = fold(grad_tail, 1, line_flips[:1])
    grad_tail, normed_back, grad_up = lax.optimization_barrier((grad_tail, normed_back, grad_up))
    grad_tail = fold(grad_tail, 1, line_flips[1:]).reshape(TEAM, rows, 4 * DQ + PAD)
    normed_back = sum(part.astype(jnp.float32) for part in normed_back)
    normed_back, feed_out = normed_back[:slots], normed_back[slots:]
    mixed = (middle + keeper * feed_out).astype(jnp.bfloat16)
    unit_one_back = normed_back * gain_one
    inputs_back = middle_back + own_scale * (
        unit_one_back - own_unit * jnp.mean(unit_one_back * own_unit, axis=-1, keepdims=True)
    )
    token_grad = inputs_back.astype(jnp.bfloat16)

    split = 3 * DQ + PAD
    grad_out = grad_tail[:, :, split:].transpose(1, 0, 2).astype(jnp.float32).reshape(-1)
    grad_last = [grad_tail[:, :, :split], grad_gate.reshape(TEAM, rows, FQ)]
    grad_last = jnp.concatenate(grad_last + [grad_up.reshape(TEAM, rows, FQ)], axis=2)
    grad_last = swap(pick(grad_last, 0))
    small_grad = sum(part[:, 3 * DQ : 3 * DQ + SMALL].astype(jnp.float32) for part in grad_last)
    small_grad = small_grad.reshape(-1)

    def columns(parts, groups, width):
        ordered = in_order(parts).astype(jnp.float32).reshape(TEAM, rows, groups, width)
        return ordered.transpose(1, 2, 0, 3).reshape(-1)

    param_grad = jnp.concatenate(
        [
            columns([part[:, : 3 * DQ] for part in grad_last], 3, DQ),
            grad_out,
            columns([part[:, split:] for part in grad_last], 2, FQ),
            grad_down.astype(jnp.float32).reshape(-1),
            small_grad,
        ]
    )
    shard_len = params.shape[0]
    matrix_mask = (jnp.arange(shard_len) < starts[4]).astype(jnp.float32)
    moment = first_decay * first_moment + (1.0 - first_decay) * param_grad
    second_new = second_decay * second_moment + (1.0 - second_decay) * param_grad * param_grad
    moment_hat = moment / (1.0 - first_decay**STEP)
    second_hat = second_new / (1.0 - second_decay**STEP)
    params_new = params - learn_rate * (
        moment_hat / (jnp.sqrt(second_hat) + moment_epsilon) + weight_decay * matrix_mask * params
    )
    return (mixed, token_grad, param_grad, small_grad, second_new, params_new)


def solution(mesh):
    placed = (
        P(AXES, None),
        P(AXES, None),
        P(),
        P(),
        P(),
        P(AXES),
        P(AXES),
        P(AXES),
    )
    return jax.shard_map(
        local,
        mesh=mesh,
        in_specs=placed,
        out_specs=(P(AXES, None), P(AXES, None), P(AXES), P(AXES), P(AXES), P(AXES)),
        check_vma=False,
    )
```

```python
import jax
import jax.numpy as jnp
from jax import lax
from jax.sharding import PartitionSpec as P

D = 1024
FF = 4608
STEP = 10
AXES = ("rep", "zero")
TEAM = 4
DQ = D // TEAM
FQ = FF // TEAM
SMALL = 5
PAD = 128

norm_epsilon = 1e-05
first_decay = 0.9
second_decay = 0.999
moment_epsilon = 1e-08
weight_decay = 0.1
learn_rate = 0.06


def rms_scale(values):
    return lax.rsqrt(jnp.mean(values * values, axis=-1, keepdims=True) + norm_epsilon)


def shift_down(values, steps):
    return jnp.pad(values, ((steps, 0), (0, 0)))[: values.shape[0]]


def shift_up(values, steps):
    return jnp.pad(values, ((0, steps), (0, 0)))[steps:]


def matmul(left, right):
    return jnp.dot(left, right, preferred_element_type=jnp.float32)


def over_rows(left, right):
    return lax.dot_general(
        left, right, (((0,), (0,)), ((), ())), preferred_element_type=jnp.float32
    )


def against(left, right):
    return lax.dot_general(
        left, right, (((1,), (1,)), ((), ())), preferred_element_type=jnp.float32
    )


def slot_masks(seq_len, seq_dev, seq_off, owners, slots):
    index = jnp.arange(slots, dtype=jnp.int32)[None, :, None]
    mine = seq_dev[None, None, :] == owners[:, None, None]
    start = seq_off[None, None, :]
    covers = mine & (index >= start) & (index < start + seq_len[None, None, :])
    live = jnp.any(covers, axis=-1)
    opening = jnp.sum(jnp.where(covers, start, 0), axis=-1)
    position = index[:, :, 0] - opening
    column = lambda flags: flags.astype(jnp.float32).reshape(-1, 1)
    return column(live), column(live & (position >= 1)), column(live & (position >= 2))


def local(tokens, cotangent, seq_len, seq_dev, seq_off, params, first_moment, second_moment):
    shards = lax.axis_size(AXES)
    line = lax.axis_size("zero")
    device = lax.axis_index(AXES)
    ring = shards // TEAM
    quarter = device // ring
    slots = tokens.shape[0]
    rings = [[q * ring + w for w in range(ring)] for q in range(TEAM)]
    peers = [quarter ^ j for j in range(TEAM)]

    def send(value, flip):
        return lax.ppermute(value, AXES, [(k, k ^ flip) for k in range(shards)])

    def spread(value):
        half = value.shape[0] // 2
        beside, above = send(value, ring), send(value, 2 * ring)
        across = [send(above[:half], ring), send(beside[half:], 2 * ring)]
        return [value, beside, above, jnp.concatenate(across, axis=0)]

    def shed(blocks):
        half = blocks[3].shape[0] // 2
        upper, lower = send(blocks[3][:half], ring), send(blocks[3][half:], 2 * ring)
        wide = [block.astype(jnp.float32) for block in (blocks[1], blocks[2], upper, lower)]
        beside = jnp.concatenate([wide[0][:half], wide[0][half:] + wide[3]], axis=0)
        above = jnp.concatenate([wide[1][:half] + wide[2], wide[1][half:]], axis=0)
        return blocks[0], beside.astype(jnp.bfloat16), above.astype(jnp.bfloat16)

    def merge(own, beside, above):
        return own, send(beside, ring), send(above, 2 * ring)

    def total(parts):
        return sum(part.astype(jnp.float32) for part in parts)

    def swap(blocks):
        return [blocks[0]] + [send(blocks[j], j * ring) for j in range(1, TEAM)]

    def in_order(pieces):
        odd, high = quarter % 2 == 1, quarter // 2 == 1
        low = [jnp.where(odd, pieces[i ^ 1], pieces[i]) for i in range(TEAM)]
        return jnp.stack([jnp.where(high, low[i ^ 2], low[i]) for i in range(TEAM)])

    def take(table, index, axis):
        return lax.dynamic_index_in_dim(table, index, axis=axis, keepdims=False)

    def pick(table, axis):
        return [take(table, peer, axis) for peer in peers]

    def after(value, earlier):
        return lax.optimization_barrier((value, earlier))

    def ring_gather(value, axis):
        return lax.all_gather(value, AXES, axis=axis, tiled=True, axis_index_groups=rings)

    core_flips = [ring >> i for i in range(1, ring.bit_length()) if ring >> i >= line]
    line_flips = [1 << i for i in range(line.bit_length() - 1)]

    def fold(value, axis, flips):
        for flip in flips:
            shape = value.shape
            half = shape[axis] // 2
            cut, place = ((2, half), axis) if flip >= line else ((half, 2), axis + 1)
            value = value.reshape(shape[:axis] + cut + shape[axis + 1 :])
            bit = (device // flip) % 2
            other = send(take(value, 1 - bit, place), flip)
            value = take(value, bit, place).astype(jnp.float32) + other.astype(jnp.float32)
            value = value.astype(jnp.bfloat16)
        return value

    rows = D // shards
    sizes = (rows * 3 * D, rows * D, rows * 2 * FF, FF // shards * D, SMALL * rows)
    starts = [sum(sizes[:i]) for i in range(6)]
    share = [params[starts[i] : starts[i + 1]] for i in range(5)]
    low = [part.astype(jnp.bfloat16) for part in share]

    deep = FF // shards
    block_small = jnp.pad(low[4].reshape(rows, SMALL), ((0, 0), (0, PAD - SMALL)))
    block_in = pick(low[0].reshape(rows, 3, TEAM, DQ), 2)
    block_in = [jnp.concatenate([b.reshape(rows, 3 * DQ), block_small], axis=1) for b in block_in]
    block_in = swap(block_in)
    block_in[1], own_tokens = after(block_in[1], tokens)
    token_parts = spread(own_tokens)
    block_out = low[1].reshape(rows, TEAM, DQ).transpose(1, 0, 2)
    ring_in = ring_gather(jnp.concatenate([in_order(block_in), block_out], axis=2), 1)

    token_parts[1], (token_parts[2], block_gu) = after(token_parts[1], (token_parts[2], low[2]))
    block_gu = pick(block_gu.reshape(rows, 2, TEAM, FQ), 2)
    block_gu = in_order(swap([b.reshape(rows, 2 * FQ) for b in block_gu]))
    weight_gateup = ring_gather(block_gu, 1).reshape(D, 2 * FQ)
    weight_down = ring_gather(low[3].reshape(deep, D), 0)
    weight_out = ring_in[:, :, 3 * DQ + PAD :].transpose(1, 0, 2).reshape(DQ, D)
    weight_out = spread(weight_out)
    weight_in = ring_in[:, :, : 3 * DQ].reshape(D, 3 * DQ)
    small = ring_in[:, :, 3 * DQ : 3 * DQ + SMALL].astype(jnp.float32).reshape(SMALL, D)
    gain_one = small[0]
    gain_two = small[1]
    taps = lax.dynamic_slice(small, (2, quarter * DQ), (3, DQ))

    owners = jnp.stack([peer * ring + device % ring for peer in peers])
    live, reach_one, reach_two = slot_masks(seq_len, seq_dev, seq_off, owners, slots)
    keeper = live[:slots]

    inputs = jnp.concatenate(token_parts, axis=0).astype(jnp.float32)
    unit_one = inputs * rms_scale(inputs)
    normed = (unit_one * gain_one).astype(jnp.bfloat16)
    mixin = matmul(normed, weight_in)
    b_part = mixin[:, :DQ]
    c_part = mixin[:, DQ : 2 * DQ]
    v_part = mixin[:, 2 * DQ :]
    product = b_part * v_part
    lag_one = shift_down(product, 1) * reach_one
    lag_two = shift_down(product, 2) * reach_two
    convolved = taps[0] * product + taps[1] * lag_one + taps[2] * lag_two
    gated = (c_part * convolved).astype(jnp.bfloat16)
    gated = swap([gated[j * slots : (j + 1) * slots] for j in range(TEAM)])

    own = tokens.astype(jnp.float32)
    own_scale = rms_scale(own)
    own_unit = own * own_scale
    branch = sum(matmul(gated[j], weight_out[j]) for j in range(TEAM))
    middle = own + keeper * branch
    scale_two = rms_scale(middle)
    unit_two = middle * scale_two
    normed_two = (unit_two * gain_two).astype(jnp.bfloat16)
    normed_two = spread(normed_two)
    normed_two, late_cotangent = after(normed_two, cotangent)
    cotangent_parts = spread(late_cotangent)
    normed_two = jnp.concatenate(normed_two, axis=0)

    upstream = jnp.concatenate(cotangent_parts, axis=0).astype(jnp.float32)
    feed_back = (live * upstream).astype(jnp.bfloat16)
    gate_up = matmul(normed_two, weight_gateup)
    gate_part = gate_up[:, :FQ]
    up_part = gate_up[:, FQ:]
    sigma = jax.nn.sigmoid(gate_part)
    swish = gate_part * sigma
    hidden = (swish * up_part).astype(jnp.bfloat16)
    hidden_back = against(feed_back, weight_down)
    gate_back = hidden_back * up_part * (sigma + gate_part * sigma * (1.0 - sigma))
    up_back = hidden_back * swish
    gateup_back = jnp.concatenate([gate_back, up_back], axis=1).astype(jnp.bfloat16)

    spans = [slice(j * slots, (j + 1) * slots) for j in range(TEAM)]
    normed_two_back = against(gateup_back, weight_gateup).astype(jnp.bfloat16)
    normed_two_back = [normed_two_back[span] for span in spans]
    normed_two_back, hidden = after(normed_two_back, hidden)
    grad_down = over_rows(hidden, feed_back).astype(jnp.bfloat16)
    grad_down = fold(grad_down.reshape(ring, deep, D), 0, core_flips)
    normed_two_back, normed_two = after(shed(normed_two_back), normed_two)
    normed_two_back = merge(*normed_two_back)
    grad_gate = over_rows(normed_two, gateup_back[:, :FQ]).astype(jnp.bfloat16)
    grad_gate = fold(grad_gate.reshape(TEAM, ring, rows, FQ), 1, core_flips)
    normed_two_back, grad_down = after(normed_two_back, grad_down)
    grad_down = fold(grad_down, 0, line_flips[:1])
    normed_two_back = total(normed_two_back)

    grad_gain_two = jnp.sum(normed_two_back * unit_two, axis=0)
    unit_two_back = normed_two_back * gain_two
    own_back = cotangent.astype(jnp.float32)
    middle_back = own_back + scale_two * (
        unit_two_back - unit_two * jnp.mean(unit_two_back * unit_two, axis=-1, keepdims=True)
    )
    branch_back = (keeper * middle_back).astype(jnp.bfloat16)
    gated_back = [against(branch_back, weight_out[j]).astype(jnp.bfloat16) for j in range(TEAM)]
    gated_back, (gated, branch_back) = after(gated_back, (gated, branch_back))
    gated_back = swap(gated_back)
    grad_out = shed([over_rows(gated[j], branch_back).astype(jnp.bfloat16) for j in range(TEAM)])
    gated_back[1], (normed_two, hidden) = after(gated_back[1], (normed_two, hidden))
    grad_up = over_rows(normed_two, gateup_back[:, FQ:]).astype(jnp.bfloat16)
    grad_up = fold(grad_up.reshape(TEAM, ring, rows, FQ), 1, core_flips)
    feed_out = matmul(hidden, weight_down).astype(jnp.bfloat16)
    gated_back, (grad_down, grad_gate) = after(gated_back, (grad_down, grad_gate))
    gated_back = jnp.concatenate(gated_back, axis=0).astype(jnp.float32)
    grad_down = fold(grad_down, 0, line_flips[1:])
    grad_gate = fold(grad_gate, 1, line_flips[:1])
    grad_out = merge(*grad_out)

    conv_back = gated_back * c_part
    c_back = gated_back * convolved
    grad_taps = jnp.stack(
        [
            jnp.sum(conv_back * product, axis=0),
            jnp.sum(conv_back * lag_one, axis=0),
            jnp.sum(conv_back * lag_two, axis=0),
        ]
    )
    product_back = (
        taps[0] * conv_back
        + shift_up(taps[1] * conv_back * reach_one, 1)
        + shift_up(taps[2] * conv_back * reach_two, 2)
    )
    mixin_back = jnp.concatenate(
        [product_back * v_part, c_back, product_back * b_part], axis=1
    ).astype(jnp.bfloat16)
    normed_back = against(mixin_back, weight_in)
    grad_gain_one = jnp.sum(normed_back * unit_one, axis=0)
    normed_back = normed_back.astype(jnp.bfloat16)
    normed_back = shed([normed_back[span] for span in spans])
    normed_back, (grad_down, grad_gate, grad_up) = after(
        normed_back, (grad_down, grad_gate, grad_up)
    )
    grad_out = total(grad_out).astype(jnp.bfloat16)
    normed_back = merge(*normed_back)
    feed_out = shed([feed_out[span] for span in spans])
    grad_gate = fold(grad_gate, 1, line_flips[1:])
    grad_up = fold(grad_up, 1, line_flips[:1])

    small_terms = lax.dynamic_update_slice(
        jnp.zeros((SMALL, D), jnp.float32), grad_taps, (2, quarter * DQ)
    )
    small_terms = small_terms.at[0].set(grad_gain_one).at[1].set(grad_gain_two)
    small_terms = jnp.pad(small_terms.reshape(D, SMALL), ((0, 0), (0, PAD - SMALL)))
    grad_tail = [
        over_rows(normed, mixin_back).astype(jnp.bfloat16).reshape(TEAM, ring, rows, 3 * DQ),
        small_terms.astype(jnp.bfloat16).reshape(TEAM, ring, rows, PAD),
        grad_out.reshape(ring, rows, TEAM, DQ).transpose(2, 0, 1, 3),
    ]
    grad_tail = jnp.concatenate(grad_tail, axis=3)
    grad_tail = fold(grad_tail, 1, core_flips)
    grad_tail, (grad_gate, grad_up) = after(grad_tail, (grad_gate, grad_up))
    grad_tail = fold(grad_tail, 1, line_flips[:1])
    grad_up = fold(grad_up, 1, line_flips[1:])
    grad_tail, (grad_up, normed_back, feed_out) = after(
        grad_tail, (grad_up, normed_back, feed_out)
    )
    grad_tail = fold(grad_tail, 1, line_flips[1:]).reshape(TEAM, rows, 4 * DQ + PAD)
    feed_out = total(merge(*feed_out))
    mixed = (middle + keeper * feed_out).astype(jnp.bfloat16)
    normed_back = total(normed_back)
    unit_one_back = normed_back * gain_one
    inputs_back = middle_back + own_scale * (
        unit_one_back - own_unit * jnp.mean(unit_one_back * own_unit, axis=-1, keepdims=True)
    )
    token_grad = inputs_back.astype(jnp.bfloat16)

    split = 3 * DQ + PAD
    grad_out = grad_tail[:, :, split:].transpose(1, 0, 2).astype(jnp.float32).reshape(-1)
    grad_last = [grad_tail[:, :, :split], grad_gate.reshape(TEAM, rows, FQ)]
    grad_last = jnp.concatenate(grad_last + [grad_up.reshape(TEAM, rows, FQ)], axis=2)
    grad_last = swap(pick(grad_last, 0))
    small_grad = sum(part[:, 3 * DQ : 3 * DQ + SMALL].astype(jnp.float32) for part in grad_last)
    small_grad = small_grad.reshape(-1)

    def columns(parts, groups, width):
        ordered = in_order(parts).astype(jnp.float32).reshape(TEAM, rows, groups, width)
        return ordered.transpose(1, 2, 0, 3).reshape(-1)

    param_grad = jnp.concatenate(
        [
            columns([part[:, : 3 * DQ] for part in grad_last], 3, DQ),
            grad_out,
            columns([part[:, split:] for part in grad_last], 2, FQ),
            grad_down.astype(jnp.float32).reshape(-1),
            small_grad,
        ]
    )
    shard_len = params.shape[0]
    matrix_mask = (jnp.arange(shard_len) < starts[4]).astype(jnp.float32)
    moment = first_decay * first_moment + (1.0 - first_decay) * param_grad
    second_new = second_decay * second_moment + (1.0 - second_decay) * param_grad * param_grad
    moment_hat = moment / (1.0 - first_decay**STEP)
    second_hat = second_new / (1.0 - second_decay**STEP)
    params_new = params - learn_rate * (
        moment_hat / (jnp.sqrt(second_hat) + moment_epsilon) + weight_decay * matrix_mask * params
    )
    return (mixed, token_grad, param_grad, small_grad, second_new, params_new)


def solution(mesh):
    placed = (
        P(AXES, None),
        P(AXES, None),
        P(),
        P(),
        P(),
        P(AXES),
        P(AXES),
        P(AXES),
    )
    return jax.shard_map(
        local,
        mesh=mesh,
        in_specs=placed,
        out_specs=(P(AXES, None), P(AXES, None), P(AXES), P(AXES), P(AXES), P(AXES)),
        check_vma=False,
    )
```

```python
import jax
import jax.numpy as jnp
from jax import lax
from jax.sharding import PartitionSpec as P

D = 1024
FF = 4608
STEP = 10
AXES = ("rep", "zero")
TEAM = 4
DQ = D // TEAM
FQ = FF // TEAM
SMALL = 5
PAD = 128

norm_epsilon = 1e-05
first_decay = 0.9
second_decay = 0.999
moment_epsilon = 1e-08
weight_decay = 0.1
learn_rate = 0.06


def rms_scale(values):
    return lax.rsqrt(jnp.mean(values * values, axis=-1, keepdims=True) + norm_epsilon)


def shift_down(values, steps):
    return jnp.pad(values, ((steps, 0), (0, 0)))[: values.shape[0]]


def shift_up(values, steps):
    return jnp.pad(values, ((0, steps), (0, 0)))[steps:]


def matmul(left, right):
    return jnp.dot(left, right, preferred_element_type=jnp.float32)


def over_rows(left, right):
    return lax.dot_general(
        left, right, (((0,), (0,)), ((), ())), preferred_element_type=jnp.float32
    )


def against(left, right):
    return lax.dot_general(
        left, right, (((1,), (1,)), ((), ())), preferred_element_type=jnp.float32
    )


def slot_masks(seq_len, seq_dev, seq_off, owners, slots):
    index = jnp.arange(slots, dtype=jnp.int32)[None, :, None]
    mine = seq_dev[None, None, :] == owners[:, None, None]
    start = seq_off[None, None, :]
    covers = mine & (index >= start) & (index < start + seq_len[None, None, :])
    live = jnp.any(covers, axis=-1)
    opening = jnp.sum(jnp.where(covers, start, 0), axis=-1)
    position = index[:, :, 0] - opening
    column = lambda flags: flags.astype(jnp.float32).reshape(-1, 1)
    return column(live), column(live & (position >= 1)), column(live & (position >= 2))


def local(tokens, cotangent, seq_len, seq_dev, seq_off, params, first_moment, second_moment):
    shards = lax.axis_size(AXES)
    line = lax.axis_size("zero")
    device = lax.axis_index(AXES)
    ring = shards // TEAM
    quarter = device >> (ring.bit_length() - 1)
    slots = tokens.shape[0]
    rings = [[q * ring + w for w in range(ring)] for q in range(TEAM)]
    peers = [quarter ^ j for j in range(TEAM)]

    def send(value, flip):
        return lax.ppermute(value, AXES, [(k, k ^ flip) for k in range(shards)])

    def reach(value):
        return value, send(value, ring), send(value, 2 * ring)

    def cross(value, beside, above):
        half = value.shape[0] // 2
        across = [send(above[:half], ring), send(beside[half:], 2 * ring)]
        return [value, beside, above, jnp.concatenate(across, axis=0)]

    def spread(value):
        return cross(*reach(value))

    def shed(blocks):
        half = blocks[3].shape[0] // 2
        return blocks, send(blocks[3][:half], ring), send(blocks[3][half:], 2 * ring)

    def join(blocks, upper, lower):
        half = upper.shape[0]
        wide = [block.astype(jnp.float32) for block in (blocks[1], blocks[2], upper, lower)]
        beside = jnp.concatenate([wide[0][:half], wide[0][half:] + wide[3]], axis=0)
        above = jnp.concatenate([wide[1][:half] + wide[2], wide[1][half:]], axis=0)
        return blocks[0], beside.astype(jnp.bfloat16), above.astype(jnp.bfloat16)

    def merge(own, beside, above):
        return own, send(beside, ring), send(above, 2 * ring)

    def total(parts):
        return sum(part.astype(jnp.float32) for part in parts)

    def swap(blocks):
        return [blocks[0]] + [send(blocks[j], j * ring) for j in range(1, TEAM)]

    def in_order(pieces):
        odd, high = (quarter & 1) == 1, (quarter >> 1) == 1
        low = [jnp.where(odd, pieces[i ^ 1], pieces[i]) for i in range(TEAM)]
        return jnp.stack([jnp.where(high, low[i ^ 2], low[i]) for i in range(TEAM)])

    def take(table, index, axis):
        return lax.dynamic_index_in_dim(
            table, index, axis=axis, keepdims=False, allow_negative_indices=False
        )

    def pick(table, axis):
        return [take(table, peer, axis) for peer in peers]

    def after(value, earlier):
        return lax.optimization_barrier((value, earlier))

    def ring_gather(value, axis):
        return lax.all_gather(value, AXES, axis=axis, tiled=True, axis_index_groups=rings)

    core_flips = [ring >> i for i in range(1, ring.bit_length()) if ring >> i >= line]
    line_flips = [1 << i for i in range(line.bit_length() - 1)]

    def line_sum(value, axis):
        return lax.psum_scatter(value, "zero", scatter_dimension=axis, tiled=True)

    def fold(value, axis, flips):
        for flip in flips:
            shape = value.shape
            half = shape[axis] // 2
            cut, place = ((2, half), axis) if flip >= line else ((half, 2), axis + 1)
            value = value.reshape(shape[:axis] + cut + shape[axis + 1 :])
            bit = (device >> (flip.bit_length() - 1)) & 1
            other = send(take(value, 1 - bit, place), flip)
            value = take(value, bit, place).astype(jnp.float32) + other.astype(jnp.float32)
            value = value.astype(jnp.bfloat16)
        return value

    rows = D // shards
    sizes = (rows * 3 * D, rows * D, rows * 2 * FF, FF // shards * D, SMALL * rows)
    starts = [sum(sizes[:i]) for i in range(6)]
    share = [params[starts[i] : starts[i + 1]] for i in range(5)]
    low = [part.astype(jnp.bfloat16) for part in share]

    deep = FF // shards
    block_small = jnp.pad(low[4].reshape(rows, SMALL), ((0, 0), (0, PAD - SMALL)))
    block_in = pick(low[0].reshape(rows, 3, TEAM, DQ), 2)
    block_in = [jnp.concatenate([b.reshape(rows, 3 * DQ), block_small], axis=1) for b in block_in]
    block_in = swap(block_in)
    block_in[1], own_tokens = after(block_in[1], tokens)
    token_parts = spread(own_tokens)
    block_out = low[1].reshape(rows, TEAM, DQ).transpose(1, 0, 2)
    ring_in = ring_gather(jnp.concatenate([in_order(block_in), block_out], axis=2), 1)

    token_parts[1], (token_parts[2], block_gu) = after(token_parts[1], (token_parts[2], low[2]))
    block_gu = pick(block_gu.reshape(rows, 2, TEAM, FQ), 2)
    block_gu = in_order(swap([b.reshape(rows, 2 * FQ) for b in block_gu]))
    weight_gateup = ring_gather(block_gu, 1).reshape(D, 2 * FQ)
    weight_down = ring_gather(low[3].reshape(deep, D), 0)
    weight_out = ring_in[:, :, 3 * DQ + PAD :].transpose(1, 0, 2).reshape(DQ, D)
    weight_out = spread(weight_out)
    weight_in = ring_in[:, :, : 3 * DQ].reshape(D, 3 * DQ)
    small = ring_in[:, :, 3 * DQ : 3 * DQ + SMALL].astype(jnp.float32).reshape(SMALL, D)
    gain_one = small[0]
    gain_two = small[1]
    taps = lax.dynamic_slice(small, (2, quarter * DQ), (3, DQ))

    owners = jnp.stack([device ^ (j * ring) for j in range(TEAM)])
    live, reach_one, reach_two = slot_masks(seq_len, seq_dev, seq_off, owners, slots)
    keeper = live[:slots]

    inputs = jnp.concatenate(token_parts, axis=0).astype(jnp.float32)
    unit_one = inputs * rms_scale(inputs)
    normed = (unit_one * gain_one).astype(jnp.bfloat16)
    mixin = matmul(normed, weight_in)
    b_part = mixin[:, :DQ]
    c_part = mixin[:, DQ : 2 * DQ]
    v_part = mixin[:, 2 * DQ :]
    product = b_part * v_part
    lag_one = shift_down(product, 1) * reach_one
    lag_two = shift_down(product, 2) * reach_two
    convolved = taps[0] * product + taps[1] * lag_one + taps[2] * lag_two
    gated = (c_part * convolved).astype(jnp.bfloat16)
    gated = swap([gated[j * slots : (j + 1) * slots] for j in range(TEAM)])

    own = tokens.astype(jnp.float32)
    own_scale = rms_scale(own)
    own_unit = own * own_scale
    branch = sum(matmul(gated[j], weight_out[j]) for j in range(TEAM))
    middle = own + keeper * branch
    scale_two = rms_scale(middle)
    unit_two = middle * scale_two
    normed_two = (unit_two * gain_two).astype(jnp.bfloat16)
    normed_two = spread(normed_two)
    normed_two, late_cotangent = after(normed_two, cotangent)
    normed_two = jnp.concatenate(normed_two, axis=0)
    cotangent_parts = reach(late_cotangent)
    gate_up = matmul(normed_two, weight_gateup)
    gate_up, cotangent_parts = after(gate_up, cotangent_parts)
    upstream = jnp.concatenate(cross(*cotangent_parts), axis=0).astype(jnp.float32)
    feed_back = (live * upstream).astype(jnp.bfloat16)
    gate_part = gate_up[:, :FQ]
    up_part = gate_up[:, FQ:]
    sigma = jax.nn.sigmoid(gate_part)
    swish = gate_part * sigma
    hidden = (swish * up_part).astype(jnp.bfloat16)
    hidden_back = against(feed_back, weight_down)
    gate_back = hidden_back * up_part * (sigma + gate_part * sigma * (1.0 - sigma))
    up_back = hidden_back * swish
    gateup_back = jnp.concatenate([gate_back, up_back], axis=1).astype(jnp.bfloat16)

    spans = [slice(j * slots, (j + 1) * slots) for j in range(TEAM)]
    normed_two_back = against(gateup_back, weight_gateup).astype(jnp.bfloat16)
    normed_two_back = [normed_two_back[span] for span in spans]
    normed_two_back, hidden = after(normed_two_back, hidden)
    grad_down = over_rows(hidden, feed_back).astype(jnp.bfloat16)
    grad_down = fold(grad_down.reshape(ring, deep, D), 0, core_flips)
    normed_two_back, normed_two = after(join(*shed(normed_two_back)), normed_two)
    normed_two_back = merge(*normed_two_back)
    grad_gate = over_rows(normed_two, gateup_back[:, :FQ]).astype(jnp.bfloat16)
    grad_gate = fold(grad_gate.reshape(TEAM, ring, rows, FQ), 1, core_flips)
    normed_two_back, grad_down = after(normed_two_back, grad_down)
    grad_down = line_sum(grad_down.reshape(line * deep, D), 0)
    normed_two_back = total(normed_two_back)

    grad_gain_two = jnp.sum(normed_two_back * unit_two, axis=0)
    unit_two_back = normed_two_back * gain_two
    own_back = cotangent.astype(jnp.float32)
    middle_back = own_back + scale_two * (
        unit_two_back - unit_two * jnp.mean(unit_two_back * unit_two, axis=-1, keepdims=True)
    )
    branch_back = (keeper * middle_back).astype(jnp.bfloat16)
    gated_back = [against(branch_back, weight_out[j]).astype(jnp.bfloat16) for j in range(TEAM)]
    gated_back, (gated, branch_back) = after(gated_back, (gated, branch_back))
    gated_back = swap(gated_back)
    grad_out = shed([over_rows(gated[j], branch_back).astype(jnp.bfloat16) for j in range(TEAM)])
    gated_back, grad_gate = after(gated_back, grad_gate)
    grad_gate = line_sum(grad_gate.reshape(TEAM, line * rows, FQ), 1)
    gated_back = jnp.concatenate(gated_back, axis=0).astype(jnp.float32)

    conv_back = gated_back * c_part
    c_back = gated_back * convolved
    grad_taps = jnp.stack(
        [
            jnp.sum(conv_back * product, axis=0),
            jnp.sum(conv_back * lag_one, axis=0),
            jnp.sum(conv_back * lag_two, axis=0),
        ]
    )
    grad_taps, grad_out = after(grad_taps, grad_out)
    grad_out = merge(*join(*grad_out))
    product_back = (
        taps[0] * conv_back
        + shift_up(taps[1] * conv_back * reach_one, 1)
        + shift_up(taps[2] * conv_back * reach_two, 2)
    )
    mixin_back = jnp.concatenate(
        [product_back * v_part, c_back, product_back * b_part], axis=1
    ).astype(jnp.bfloat16)
    mixin_back, normed_two = after(mixin_back, normed_two)
    grad_up = over_rows(normed_two, gateup_back[:, FQ:]).astype(jnp.bfloat16)
    grad_up = fold(grad_up.reshape(TEAM, ring, rows, FQ), 1, core_flips)
    grad_in = over_rows(normed, mixin_back).astype(jnp.bfloat16)
    grad_in, (hidden, grad_up, grad_down) = after(grad_in, (hidden, grad_up, grad_down))
    grad_up = line_sum(grad_up.reshape(TEAM, line * rows, FQ), 1)
    feed_out = matmul(hidden, weight_down).astype(jnp.bfloat16)
    normed_back = against(mixin_back, weight_in)
    grad_gain_one = jnp.sum(normed_back * unit_one, axis=0)
    normed_back = normed_back.astype(jnp.bfloat16)
    normed_back = [normed_back[span] for span in spans]
    grad_out = total(grad_out).astype(jnp.bfloat16)
    normed_back, feed_out = after(join(*shed(normed_back)), feed_out)
    feed_out = shed([feed_out[span] for span in spans])

    small_terms = lax.dynamic_update_slice(
        jnp.zeros((SMALL, D), jnp.float32), grad_taps, (2, quarter * DQ)
    )
    small_terms = small_terms.at[0].set(grad_gain_one).at[1].set(grad_gain_two)
    small_terms = jnp.pad(small_terms.reshape(D, SMALL), ((0, 0), (0, PAD - SMALL)))
    grad_tail = [
        grad_in.reshape(TEAM, ring, rows, 3 * DQ),
        small_terms.astype(jnp.bfloat16).reshape(TEAM, ring, rows, PAD),
        grad_out.reshape(ring, rows, TEAM, DQ).transpose(2, 0, 1, 3),
    ]
    grad_tail = jnp.concatenate(grad_tail, axis=3)
    grad_tail = fold(grad_tail, 1, core_flips)
    grad_tail, normed_back = after(grad_tail, normed_back)
    normed_back = merge(*normed_back)
    grad_tail = fold(grad_tail, 1, line_flips[:1])
    grad_tail, (grad_gate, normed_back, feed_out) = after(
        grad_tail, (grad_gate, normed_back, join(*feed_out))
    )
    feed_out = merge(*feed_out)
    grad_tail = fold(grad_tail, 1, line_flips[1:]).reshape(TEAM, rows, 4 * DQ + PAD)
    feed_out = total(feed_out)
    mixed = (middle + keeper * feed_out).astype(jnp.bfloat16)
    normed_back = total(normed_back)
    unit_one_back = normed_back * gain_one
    inputs_back = middle_back + own_scale * (
        unit_one_back - own_unit * jnp.mean(unit_one_back * own_unit, axis=-1, keepdims=True)
    )
    token_grad = inputs_back.astype(jnp.bfloat16)

    split = 3 * DQ + PAD
    grad_out = grad_tail[:, :, split:].transpose(1, 0, 2).astype(jnp.float32).reshape(-1)
    grad_in = swap(pick(grad_tail[:, :, :split], 0))
    grad_last = jnp.concatenate([grad_gate, grad_up], axis=2)
    grad_last = swap(pick(grad_last, 0))
    small_grad = sum(part[:, 3 * DQ : 3 * DQ + SMALL].astype(jnp.float32) for part in grad_in)
    small_grad = small_grad.reshape(-1)

    def columns(parts, groups, width):
        ordered = in_order(parts).astype(jnp.float32).reshape(TEAM, rows, groups, width)
        return ordered.transpose(1, 2, 0, 3).reshape(-1)

    param_grad = jnp.concatenate(
        [
            columns([part[:, : 3 * DQ] for part in grad_in], 3, DQ),
            grad_out,
            columns(grad_last, 2, FQ),
            grad_down.astype(jnp.float32).reshape(-1),
            small_grad,
        ]
    )
    shard_len = params.shape[0]
    matrix_mask = (jnp.arange(shard_len) < starts[4]).astype(jnp.float32)
    moment = first_decay * first_moment + (1.0 - first_decay) * param_grad
    second_new = second_decay * second_moment + (1.0 - second_decay) * param_grad * param_grad
    moment_hat = moment / (1.0 - first_decay**STEP)
    second_hat = second_new / (1.0 - second_decay**STEP)
    params_new = params - learn_rate * (
        moment_hat / (jnp.sqrt(second_hat) + moment_epsilon) + weight_decay * matrix_mask * params
    )
    return (mixed, token_grad, param_grad, small_grad, second_new, params_new)


def solution(mesh):
    placed = (
        P(AXES, None),
        P(AXES, None),
        P(),
        P(),
        P(),
        P(AXES),
        P(AXES),
        P(AXES),
    )
    return jax.shard_map(
        local,
        mesh=mesh,
        in_specs=placed,
        out_specs=(P(AXES, None), P(AXES, None), P(AXES), P(AXES), P(AXES), P(AXES)),
        check_vma=False,
    )
```

```python
import jax
import jax.numpy as jnp
from jax import lax
from jax.sharding import PartitionSpec as P

D = 1024
FF = 4608
STEP = 10
AXES = ("rep", "zero")
TEAM = 4
DQ = D // TEAM
FQ = FF // TEAM
SMALL = 5
PAD = 128

norm_epsilon = 1e-05
first_decay = 0.9
second_decay = 0.999
moment_epsilon = 1e-08
weight_decay = 0.1
learn_rate = 0.06


def rms_scale(values):
    return lax.rsqrt(jnp.mean(values * values, axis=-1, keepdims=True) + norm_epsilon)


def shift_down(values, steps):
    return jnp.pad(values, ((steps, 0), (0, 0)))[: values.shape[0]]


def shift_up(values, steps):
    return jnp.pad(values, ((0, steps), (0, 0)))[steps:]


def matmul(left, right):
    return jnp.dot(left, right, preferred_element_type=jnp.float32)


def over_rows(left, right):
    return lax.dot_general(
        left, right, (((0,), (0,)), ((), ())), preferred_element_type=jnp.float32
    )


def against(left, right):
    return lax.dot_general(
        left, right, (((1,), (1,)), ((), ())), preferred_element_type=jnp.float32
    )


def slot_masks(seq_len, seq_dev, seq_off, owners, slots):
    index = jnp.arange(slots, dtype=jnp.int32)[None, :, None]
    mine = seq_dev[None, None, :] == owners[:, None, None]
    start = seq_off[None, None, :]
    covers = mine & (index >= start) & (index < start + seq_len[None, None, :])
    live = jnp.any(covers, axis=-1)
    opening = jnp.sum(jnp.where(covers, start, 0), axis=-1)
    position = index[:, :, 0] - opening
    column = lambda flags: flags.astype(jnp.float32).reshape(-1, 1)
    return column(live), column(live & (position >= 1)), column(live & (position >= 2))


def local(tokens, cotangent, seq_len, seq_dev, seq_off, params, first_moment, second_moment):
    shards = lax.axis_size(AXES)
    line = lax.axis_size("zero")
    device = lax.axis_index(AXES)
    ring = shards // TEAM
    quarter = device >> (ring.bit_length() - 1)
    slots = tokens.shape[0]
    rings = [[q * ring + w for w in range(ring)] for q in range(TEAM)]
    peers = [quarter ^ j for j in range(TEAM)]

    def send(value, flip):
        return lax.ppermute(value, AXES, [(k, k ^ flip) for k in range(shards)])

    def reach(value):
        return value, send(value, ring), send(value, 2 * ring)

    def cross(value, beside, above):
        half = value.shape[0] // 2
        across = [send(above[:half], ring), send(beside[half:], 2 * ring)]
        return [value, beside, above, jnp.concatenate(across, axis=0)]

    def spread(value):
        return cross(*reach(value))

    def shed(blocks):
        half = blocks[3].shape[0] // 2
        return blocks, send(blocks[3][:half], ring), send(blocks[3][half:], 2 * ring)

    def join(blocks, upper, lower):
        half = upper.shape[0]
        wide = [block.astype(jnp.float32) for block in (blocks[1], blocks[2], upper, lower)]
        beside = jnp.concatenate([wide[0][:half], wide[0][half:] + wide[3]], axis=0)
        above = jnp.concatenate([wide[1][:half] + wide[2], wide[1][half:]], axis=0)
        return blocks[0], beside.astype(jnp.bfloat16), above.astype(jnp.bfloat16)

    def merge(own, beside, above):
        return own, send(beside, ring), send(above, 2 * ring)

    def total(parts):
        return sum(part.astype(jnp.float32) for part in parts)

    def swap(blocks):
        return [blocks[0]] + [send(blocks[j], j * ring) for j in range(1, TEAM)]

    def in_order(pieces):
        odd, high = (quarter & 1) == 1, (quarter >> 1) == 1
        low = [jnp.where(odd, pieces[i ^ 1], pieces[i]) for i in range(TEAM)]
        return jnp.stack([jnp.where(high, low[i ^ 2], low[i]) for i in range(TEAM)])

    def take(table, index, axis):
        return lax.dynamic_index_in_dim(
            table, index, axis=axis, keepdims=False, allow_negative_indices=False
        )

    def pick(table, axis):
        return [take(table, peer, axis) for peer in peers]

    def after(value, earlier):
        return lax.optimization_barrier((value, earlier))

    def ring_gather(value, axis):
        return lax.all_gather(value, AXES, axis=axis, tiled=True, axis_index_groups=rings)

    core_flips = [ring >> i for i in range(1, ring.bit_length()) if ring >> i >= line]
    line_flips = [1 << i for i in range(line.bit_length() - 1)]

    def line_sum(value, axis):
        return lax.psum_scatter(value, "zero", scatter_dimension=axis, tiled=True)

    def fold(value, axis, flips):
        for flip in flips:
            shape = value.shape
            half = shape[axis] // 2
            cut, place = ((2, half), axis) if flip >= line else ((half, 2), axis + 1)
            value = value.reshape(shape[:axis] + cut + shape[axis + 1 :])
            bit = (device >> (flip.bit_length() - 1)) & 1
            other = send(take(value, 1 - bit, place), flip)
            value = take(value, bit, place).astype(jnp.float32) + other.astype(jnp.float32)
            value = value.astype(jnp.bfloat16)
        return value

    rows = D // shards
    sizes = (rows * 3 * D, rows * D, rows * 2 * FF, FF // shards * D, SMALL * rows)
    starts = [sum(sizes[:i]) for i in range(6)]
    share = [params[starts[i] : starts[i + 1]] for i in range(5)]
    low = [part.astype(jnp.bfloat16) for part in share]

    deep = FF // shards
    block_small = jnp.pad(low[4].reshape(rows, SMALL), ((0, 0), (0, PAD - SMALL)))
    block_in = pick(low[0].reshape(rows, 3, TEAM, DQ), 2)
    block_in = [jnp.concatenate([b.reshape(rows, 3 * DQ), block_small], axis=1) for b in block_in]
    block_in = swap(block_in)
    block_in[1], own_tokens = after(block_in[1], tokens)
    token_parts = spread(own_tokens)
    block_out = low[1].reshape(rows, TEAM, DQ).transpose(1, 0, 2)
    ring_in = ring_gather(jnp.concatenate([in_order(block_in), block_out], axis=2), 1)

    token_parts[1], (token_parts[2], block_gu) = after(token_parts[1], (token_parts[2], low[2]))
    block_gu = pick(block_gu.reshape(rows, 2, TEAM, FQ), 2)
    block_gu = in_order(swap([b.reshape(rows, 2 * FQ) for b in block_gu]))
    weight_gateup = ring_gather(block_gu, 1).reshape(D, 2 * FQ)
    weight_down = ring_gather(low[3].reshape(deep, D), 0)
    weight_out = ring_in[:, :, 3 * DQ + PAD :].transpose(1, 0, 2).reshape(DQ, D)
    weight_out = spread(weight_out)
    weight_in = ring_in[:, :, : 3 * DQ].reshape(D, 3 * DQ)
    small = ring_in[:, :, 3 * DQ : 3 * DQ + SMALL].astype(jnp.float32).reshape(SMALL, D)
    gain_one = small[0]
    gain_two = small[1]
    taps = lax.dynamic_slice(small, (2, quarter * DQ), (3, DQ))

    owners = jnp.stack([device ^ (j * ring) for j in range(TEAM)])
    live, reach_one, reach_two = slot_masks(seq_len, seq_dev, seq_off, owners, slots)
    keeper = live[:slots]

    inputs = jnp.concatenate(token_parts, axis=0).astype(jnp.float32)
    unit_one = inputs * rms_scale(inputs)
    normed = (unit_one * gain_one).astype(jnp.bfloat16)
    mixin = matmul(normed, weight_in)
    b_part = mixin[:, :DQ]
    c_part = mixin[:, DQ : 2 * DQ]
    v_part = mixin[:, 2 * DQ :]
    product = b_part * v_part
    lag_one = shift_down(product, 1) * reach_one
    lag_two = shift_down(product, 2) * reach_two
    convolved = taps[0] * product + taps[1] * lag_one + taps[2] * lag_two
    gated = (c_part * convolved).astype(jnp.bfloat16)
    gated = swap([gated[j * slots : (j + 1) * slots] for j in range(TEAM)])

    own = tokens.astype(jnp.float32)
    own_scale = rms_scale(own)
    own_unit = own * own_scale
    branch = sum(matmul(gated[j], weight_out[j]) for j in range(TEAM))
    middle = own + keeper * branch
    scale_two = rms_scale(middle)
    unit_two = middle * scale_two
    normed_two = (unit_two * gain_two).astype(jnp.bfloat16)
    normed_two = spread(normed_two)
    normed_two, late_cotangent = after(normed_two, cotangent)
    normed_two = jnp.concatenate(normed_two, axis=0)
    cotangent_parts = reach(late_cotangent)
    gate_up = matmul(normed_two, weight_gateup)
    gate_up, cotangent_parts = after(gate_up, cotangent_parts)
    upstream = jnp.concatenate(cross(*cotangent_parts), axis=0).astype(jnp.float32)
    feed_back = (live * upstream).astype(jnp.bfloat16)
    gate_part = gate_up[:, :FQ]
    up_part = gate_up[:, FQ:]
    sigma = jax.nn.sigmoid(gate_part)
    swish = gate_part * sigma
    hidden = (swish * up_part).astype(jnp.bfloat16)
    hidden_back = against(feed_back, weight_down)
    gate_back = hidden_back * up_part * (sigma + gate_part * sigma * (1.0 - sigma))
    up_back = hidden_back * swish
    gateup_back = jnp.concatenate([gate_back, up_back], axis=1).astype(jnp.bfloat16)

    spans = [slice(j * slots, (j + 1) * slots) for j in range(TEAM)]
    normed_two_back = against(gateup_back, weight_gateup).astype(jnp.bfloat16)
    normed_two_back = [normed_two_back[span] for span in spans]
    normed_two_back, hidden = after(normed_two_back, hidden)
    grad_down = over_rows(hidden, feed_back).astype(jnp.bfloat16)
    grad_down = fold(grad_down.reshape(ring, deep, D), 0, core_flips)
    normed_two_back, normed_two = after(join(*shed(normed_two_back)), normed_two)
    normed_two_back = merge(*normed_two_back)
    grad_gate = over_rows(normed_two, gateup_back[:, :FQ]).astype(jnp.bfloat16)
    grad_gate = fold(grad_gate.reshape(TEAM, ring, rows, FQ), 1, core_flips)
    normed_two_back, grad_down = after(normed_two_back, grad_down)
    grad_down = line_sum(grad_down.reshape(line * deep, D), 0)
    normed_two_back = total(normed_two_back)

    grad_gain_two = jnp.sum(normed_two_back * unit_two, axis=0)
    unit_two_back = normed_two_back * gain_two
    own_back = cotangent.astype(jnp.float32)
    middle_back = own_back + scale_two * (
        unit_two_back - unit_two * jnp.mean(unit_two_back * unit_two, axis=-1, keepdims=True)
    )
    branch_back = (keeper * middle_back).astype(jnp.bfloat16)
    gated_back = [against(branch_back, weight_out[j]).astype(jnp.bfloat16) for j in range(TEAM)]
    gated_back, (gated, branch_back) = after(gated_back, (gated, branch_back))
    gated_back = swap(gated_back)
    grad_out = shed([over_rows(gated[j], branch_back).astype(jnp.bfloat16) for j in range(TEAM)])
    gated_back, grad_gate = after(gated_back, grad_gate)
    grad_gate = line_sum(grad_gate.reshape(TEAM, line * rows, FQ), 1)
    gated_back = jnp.concatenate(gated_back, axis=0).astype(jnp.float32)

    conv_back = gated_back * c_part
    c_back = gated_back * convolved
    grad_taps = jnp.stack(
        [
            jnp.sum(conv_back * product, axis=0),
            jnp.sum(conv_back * lag_one, axis=0),
            jnp.sum(conv_back * lag_two, axis=0),
        ]
    )
    grad_taps, grad_out = after(grad_taps, grad_out)
    grad_out = merge(*join(*grad_out))
    product_back = (
        taps[0] * conv_back
        + shift_up(taps[1] * conv_back * reach_one, 1)
        + shift_up(taps[2] * conv_back * reach_two, 2)
    )
    mixin_back = jnp.concatenate(
        [product_back * v_part, c_back, product_back * b_part], axis=1
    ).astype(jnp.bfloat16)
    mixin_back, normed_two = after(mixin_back, normed_two)
    grad_up = over_rows(normed_two, gateup_back[:, FQ:]).astype(jnp.bfloat16)
    grad_up = fold(grad_up.reshape(TEAM, ring, rows, FQ), 1, core_flips)
    grad_in = over_rows(normed, mixin_back).astype(jnp.bfloat16)
    grad_in, (hidden, grad_up, grad_down) = after(grad_in, (hidden, grad_up, grad_down))
    grad_up = line_sum(grad_up.reshape(TEAM, line * rows, FQ), 1)
    feed_out = matmul(hidden, weight_down).astype(jnp.bfloat16)
    normed_back = against(mixin_back, weight_in)
    grad_gain_one = jnp.sum(normed_back * unit_one, axis=0)
    normed_back = normed_back.astype(jnp.bfloat16)
    normed_back = [normed_back[span] for span in spans]
    grad_out = total(grad_out).astype(jnp.bfloat16)
    normed_back, feed_out = after(join(*shed(normed_back)), feed_out)
    feed_out = shed([feed_out[span] for span in spans])

    small_terms = lax.dynamic_update_slice(
        jnp.zeros((SMALL, D), jnp.float32), grad_taps, (2, quarter * DQ)
    )
    small_terms = small_terms.at[0].set(grad_gain_one).at[1].set(grad_gain_two)
    small_terms = jnp.pad(small_terms.reshape(D, SMALL), ((0, 0), (0, PAD - SMALL)))
    grad_tail = [
        grad_in.reshape(TEAM, ring, rows, 3 * DQ),
        small_terms.astype(jnp.bfloat16).reshape(TEAM, ring, rows, PAD),
        grad_out.reshape(ring, rows, TEAM, DQ).transpose(2, 0, 1, 3),
    ]
    grad_tail = jnp.concatenate(grad_tail, axis=3)
    grad_tail = fold(grad_tail, 1, core_flips)
    grad_tail, normed_back = after(grad_tail, normed_back)
    normed_back = merge(*normed_back)
    grad_tail = fold(grad_tail, 1, line_flips[:1])
    grad_tail, (grad_gate, normed_back, feed_out) = after(
        grad_tail, (grad_gate, normed_back, join(*feed_out))
    )
    feed_out = merge(*feed_out)
    grad_tail = fold(grad_tail, 1, line_flips[1:]).reshape(TEAM, rows, 4 * DQ + PAD)
    feed_out = total(feed_out)
    mixed = (middle + keeper * feed_out).astype(jnp.bfloat16)
    normed_back = total(normed_back)
    unit_one_back = normed_back * gain_one
    inputs_back = middle_back + own_scale * (
        unit_one_back - own_unit * jnp.mean(unit_one_back * own_unit, axis=-1, keepdims=True)
    )
    token_grad = inputs_back.astype(jnp.bfloat16)

    split = 3 * DQ + PAD
    grad_last = jnp.concatenate([grad_tail[:, :, :split], grad_gate, grad_up], axis=2)
    grad_last = swap(pick(grad_last, 0))
    small_grad = sum(part[:, 3 * DQ : 3 * DQ + SMALL].astype(jnp.float32) for part in grad_last)
    small_grad = small_grad.reshape(-1)
    grad_out = grad_tail[:, :, split:].transpose(1, 0, 2).astype(jnp.float32).reshape(-1)

    def columns(parts, groups, width):
        ordered = in_order(parts).astype(jnp.float32).reshape(TEAM, rows, groups, width)
        return ordered.transpose(1, 2, 0, 3).reshape(-1)

    grads = [
        columns([part[:, : 3 * DQ] for part in grad_last], 3, DQ),
        grad_out,
        columns([part[:, split:] for part in grad_last], 2, FQ),
        grad_down.astype(jnp.float32).reshape(-1),
        small_grad,
    ]
    seconds, renewed = [], []
    for i, grad in enumerate(grads):
        span = slice(starts[i], starts[i + 1])
        moment = first_decay * first_moment[span] + (1.0 - first_decay) * grad
        second = second_decay * second_moment[span] + (1.0 - second_decay) * grad * grad
        moment_hat = moment / (1.0 - first_decay**STEP)
        second_hat = second / (1.0 - second_decay**STEP)
        decay = weight_decay if i < 4 else 0.0
        step = moment_hat / (jnp.sqrt(second_hat) + moment_epsilon) + decay * share[i]
        seconds.append(second)
        renewed.append(share[i] - learn_rate * step)
    param_grad = jnp.concatenate(grads)
    second_new = jnp.concatenate(seconds)
    params_new = jnp.concatenate(renewed)
    return (mixed, token_grad, param_grad, small_grad, second_new, params_new)


def solution(mesh):
    placed = (
        P(AXES, None),
        P(AXES, None),
        P(),
        P(),
        P(),
        P(AXES),
        P(AXES),
        P(AXES),
    )
    return jax.shard_map(
        local,
        mesh=mesh,
        in_specs=placed,
        out_specs=(P(AXES, None), P(AXES, None), P(AXES), P(AXES), P(AXES), P(AXES)),
        check_vma=False,
    )
```

```python
import jax
import jax.numpy as jnp
from jax import lax
from jax.sharding import PartitionSpec as P

D = 1024
FF = 4608
STEP = 10
AXES = ("rep", "zero")
TEAM = 4
DQ = D // TEAM
FQ = FF // TEAM
SMALL = 5
PAD = 128

norm_epsilon = 1e-05
first_decay = 0.9
second_decay = 0.999
moment_epsilon = 1e-08
weight_decay = 0.1
learn_rate = 0.06


def rms_scale(values):
    return lax.rsqrt(jnp.mean(values * values, axis=-1, keepdims=True) + norm_epsilon)


def shift_down(values, steps):
    return jnp.pad(values, ((steps, 0), (0, 0)))[: values.shape[0]]


def shift_up(values, steps):
    return jnp.pad(values, ((0, steps), (0, 0)))[steps:]


def matmul(left, right):
    return jnp.dot(left, right, preferred_element_type=jnp.float32)


def over_rows(left, right):
    return lax.dot_general(
        left, right, (((0,), (0,)), ((), ())), preferred_element_type=jnp.float32
    )


def against(left, right):
    return lax.dot_general(
        left, right, (((1,), (1,)), ((), ())), preferred_element_type=jnp.float32
    )


def slot_masks(seq_len, seq_dev, seq_off, owners, slots):
    index = jnp.arange(slots, dtype=jnp.int32)[None, :, None]
    mine = seq_dev[None, None, :] == owners[:, None, None]
    start = seq_off[None, None, :]
    covers = mine & (index >= start) & (index < start + seq_len[None, None, :])
    live = jnp.any(covers, axis=-1)
    opening = jnp.sum(jnp.where(covers, start, 0), axis=-1)
    position = index[:, :, 0] - opening
    column = lambda flags: flags.astype(jnp.float32).reshape(-1, 1)
    return column(live), column(live & (position >= 1)), column(live & (position >= 2))


def local(tokens, cotangent, seq_len, seq_dev, seq_off, params, first_moment, second_moment):
    shards = lax.axis_size(AXES)
    line = lax.axis_size("zero")
    device = lax.axis_index(AXES)
    ring = shards // TEAM
    quarter = device >> (ring.bit_length() - 1)
    slots = tokens.shape[0]
    rings = [[q * ring + w for w in range(ring)] for q in range(TEAM)]
    peers = [quarter ^ j for j in range(TEAM)]

    def send(value, flip):
        return lax.ppermute(value, AXES, [(k, k ^ flip) for k in range(shards)])

    def reach(value):
        return value, send(value, ring), send(value, 2 * ring)

    def cross(value, beside, above):
        half = value.shape[0] // 2
        across = [send(above[:half], ring), send(beside[half:], 2 * ring)]
        return [value, beside, above, jnp.concatenate(across, axis=0)]

    def spread(value):
        return cross(*reach(value))

    def shed(blocks):
        half = blocks[3].shape[0] // 2
        return blocks, send(blocks[3][:half], ring), send(blocks[3][half:], 2 * ring)

    def join(blocks, upper, lower):
        half = upper.shape[0]
        wide = [block.astype(jnp.float32) for block in (blocks[1], blocks[2], upper, lower)]
        beside = jnp.concatenate([wide[0][:half], wide[0][half:] + wide[3]], axis=0)
        above = jnp.concatenate([wide[1][:half] + wide[2], wide[1][half:]], axis=0)
        return blocks[0], beside.astype(jnp.bfloat16), above.astype(jnp.bfloat16)

    def merge(own, beside, above):
        return own, send(beside, ring), send(above, 2 * ring)

    def total(parts):
        return sum(part.astype(jnp.float32) for part in parts)

    def swap(blocks):
        return [blocks[0]] + [send(blocks[j], j * ring) for j in range(1, TEAM)]

    def in_order(pieces):
        odd, high = (quarter & 1) == 1, (quarter >> 1) == 1
        low = [jnp.where(odd, pieces[i ^ 1], pieces[i]) for i in range(TEAM)]
        return jnp.stack([jnp.where(high, low[i ^ 2], low[i]) for i in range(TEAM)])

    def take(table, index, axis):
        return lax.dynamic_index_in_dim(
            table, index, axis=axis, keepdims=False, allow_negative_indices=False
        )

    def pick(table, axis):
        return [take(table, peer, axis) for peer in peers]

    def after(value, earlier):
        return lax.optimization_barrier((value, earlier))

    def ring_gather(value, axis):
        return lax.all_gather(value, AXES, axis=axis, tiled=True, axis_index_groups=rings)

    core_flips = [ring >> i for i in range(1, ring.bit_length()) if ring >> i >= line]
    line_flips = [1 << i for i in range(line.bit_length() - 1)]

    def line_sum(value, axis):
        return lax.psum_scatter(value, "zero", scatter_dimension=axis, tiled=True)

    def fold(value, axis, flips):
        for flip in flips:
            shape = value.shape
            half = shape[axis] // 2
            cut, place = ((2, half), axis) if flip >= line else ((half, 2), axis + 1)
            value = value.reshape(shape[:axis] + cut + shape[axis + 1 :])
            bit = (device >> (flip.bit_length() - 1)) & 1
            other = send(take(value, 1 - bit, place), flip)
            value = take(value, bit, place).astype(jnp.float32) + other.astype(jnp.float32)
            value = value.astype(jnp.bfloat16)
        return value

    rows = D // shards
    sizes = (rows * 3 * D, rows * D, rows * 2 * FF, FF // shards * D, SMALL * rows)
    starts = [sum(sizes[:i]) for i in range(6)]
    share = [params[starts[i] : starts[i + 1]] for i in range(5)]
    low = [part.astype(jnp.bfloat16) for part in share]

    deep = FF // shards
    block_small = jnp.pad(low[4].reshape(rows, SMALL), ((0, 0), (0, PAD - SMALL)))
    block_in = pick(low[0].reshape(rows, 3, TEAM, DQ), 2)
    block_in = [jnp.concatenate([b.reshape(rows, 3 * DQ), block_small], axis=1) for b in block_in]
    block_in = swap(block_in)
    block_in[1], own_tokens = after(block_in[1], tokens)
    token_parts = spread(own_tokens)
    block_out = low[1].reshape(rows, TEAM, DQ).transpose(1, 0, 2)
    ring_in = ring_gather(jnp.concatenate([in_order(block_in), block_out], axis=2), 1)

    token_parts[1], (token_parts[2], block_gu) = after(token_parts[1], (token_parts[2], low[2]))
    block_gu = pick(block_gu.reshape(rows, 2, TEAM, FQ), 2)
    block_gu = in_order(swap([b.reshape(rows, 2 * FQ) for b in block_gu]))
    weight_gateup = ring_gather(block_gu, 1).reshape(D, 2 * FQ)
    weight_down = ring_gather(low[3].reshape(deep, D), 0)
    weight_out = ring_in[:, :, 3 * DQ + PAD :].transpose(1, 0, 2).reshape(DQ, D)
    weight_out = spread(weight_out)
    weight_in = ring_in[:, :, : 3 * DQ].reshape(D, 3 * DQ)
    small = ring_in[:, :, 3 * DQ : 3 * DQ + SMALL].astype(jnp.float32).reshape(SMALL, D)
    gain_one = small[0]
    gain_two = small[1]
    taps = lax.dynamic_slice(small, (2, quarter * DQ), (3, DQ))

    owners = jnp.stack([device ^ (j * ring) for j in range(TEAM)])
    live, reach_one, reach_two = slot_masks(seq_len, seq_dev, seq_off, owners, slots)
    keeper = live[:slots]

    inputs = jnp.concatenate(token_parts, axis=0).astype(jnp.float32)
    unit_one = inputs * rms_scale(inputs)
    normed = (unit_one * gain_one).astype(jnp.bfloat16)
    mixin = matmul(normed, weight_in)
    b_part = mixin[:, :DQ]
    c_part = mixin[:, DQ : 2 * DQ]
    v_part = mixin[:, 2 * DQ :]
    product = b_part * v_part
    lag_one = shift_down(product, 1) * reach_one
    lag_two = shift_down(product, 2) * reach_two
    convolved = taps[0] * product + taps[1] * lag_one + taps[2] * lag_two
    gated = (c_part * convolved).astype(jnp.bfloat16)
    gated = swap([gated[j * slots : (j + 1) * slots] for j in range(TEAM)])

    own = tokens.astype(jnp.float32)
    own_scale = rms_scale(own)
    own_unit = own * own_scale
    branch = sum(matmul(gated[j], weight_out[j]) for j in range(TEAM))
    middle = own + keeper * branch
    scale_two = rms_scale(middle)
    unit_two = middle * scale_two
    normed_two = (unit_two * gain_two).astype(jnp.bfloat16)
    normed_two = spread(normed_two)
    normed_two, late_cotangent = after(normed_two, cotangent)
    normed_two = jnp.concatenate(normed_two, axis=0)
    cotangent_parts = reach(late_cotangent)
    gate_up = matmul(normed_two, weight_gateup)
    gate_up, cotangent_parts = after(gate_up, cotangent_parts)
    upstream = jnp.concatenate(cross(*cotangent_parts), axis=0).astype(jnp.float32)
    feed_back = (live * upstream).astype(jnp.bfloat16)
    gate_part = gate_up[:, :FQ]
    up_part = gate_up[:, FQ:]
    sigma = jax.nn.sigmoid(gate_part)
    swish = gate_part * sigma
    hidden = (swish * up_part).astype(jnp.bfloat16)
    hidden_back = against(feed_back, weight_down)
    gate_back = hidden_back * up_part * (sigma + gate_part * sigma * (1.0 - sigma))
    up_back = hidden_back * swish
    gateup_back = jnp.concatenate([gate_back, up_back], axis=1).astype(jnp.bfloat16)

    spans = [slice(j * slots, (j + 1) * slots) for j in range(TEAM)]
    normed_two_back = against(gateup_back, weight_gateup).astype(jnp.bfloat16)
    normed_two_back = [normed_two_back[span] for span in spans]
    normed_two_back, hidden = after(normed_two_back, hidden)
    grad_down = over_rows(hidden, feed_back).astype(jnp.bfloat16)
    grad_down = fold(grad_down.reshape(ring, deep, D), 0, core_flips)
    normed_two_back, normed_two = after(join(*shed(normed_two_back)), normed_two)
    normed_two_back = merge(*normed_two_back)
    grad_gate = over_rows(normed_two, gateup_back[:, :FQ]).astype(jnp.bfloat16)
    grad_gate = fold(grad_gate.reshape(TEAM, ring, rows, FQ), 1, core_flips)
    normed_two_back, grad_down = after(normed_two_back, grad_down)
    grad_down = line_sum(grad_down.reshape(line * deep, D), 0)
    normed_two_back = total(normed_two_back)

    grad_gain_two = jnp.sum(normed_two_back * unit_two, axis=0)
    unit_two_back = normed_two_back * gain_two
    own_back = cotangent.astype(jnp.float32)
    middle_back = own_back + scale_two * (
        unit_two_back - unit_two * jnp.mean(unit_two_back * unit_two, axis=-1, keepdims=True)
    )
    branch_back = (keeper * middle_back).astype(jnp.bfloat16)
    gated_back = against(branch_back, jnp.concatenate(weight_out, axis=0)).astype(jnp.bfloat16)
    gated_back = [gated_back[:, j * DQ : (j + 1) * DQ] for j in range(TEAM)]
    gated_back, (gated, branch_back) = after(gated_back, (gated, branch_back))
    gated_back = swap(gated_back)
    grad_out = shed([over_rows(gated[j], branch_back).astype(jnp.bfloat16) for j in range(TEAM)])
    gated_back, grad_gate = after(gated_back, grad_gate)
    grad_gate = line_sum(grad_gate.reshape(TEAM, line * rows, FQ), 1)
    gated_back = jnp.concatenate(gated_back, axis=0).astype(jnp.float32)

    conv_back = gated_back * c_part
    c_back = gated_back * convolved
    grad_taps = jnp.stack(
        [
            jnp.sum(conv_back * product, axis=0),
            jnp.sum(conv_back * lag_one, axis=0),
            jnp.sum(conv_back * lag_two, axis=0),
        ]
    )
    grad_taps, grad_out = after(grad_taps, grad_out)
    grad_out = merge(*join(*grad_out))
    product_back = (
        taps[0] * conv_back
        + shift_up(taps[1] * conv_back * reach_one, 1)
        + shift_up(taps[2] * conv_back * reach_two, 2)
    )
    mixin_back = jnp.concatenate(
        [product_back * v_part, c_back, product_back * b_part], axis=1
    ).astype(jnp.bfloat16)
    grad_in = over_rows(normed, mixin_back).astype(jnp.bfloat16)
    grad_in, (hidden, normed_two) = after(grad_in, (hidden, normed_two))
    grad_up = over_rows(normed_two, gateup_back[:, FQ:]).astype(jnp.bfloat16)
    grad_up = fold(grad_up.reshape(TEAM, ring, rows, FQ), 1, core_flips)
    feed_out = matmul(hidden, weight_down).astype(jnp.bfloat16)
    normed_back = against(mixin_back, weight_in)
    grad_gain_one = jnp.sum(normed_back * unit_one, axis=0)
    normed_back = normed_back.astype(jnp.bfloat16)
    grad_out = total(grad_out).astype(jnp.bfloat16)
    normed_back, grad_out = after(normed_back, grad_out)
    normed_back = [normed_back[span] for span in spans]
    normed_back, feed_out = after(join(*shed(normed_back)), feed_out)
    feed_out = shed([feed_out[span] for span in spans])

    small_terms = lax.dynamic_update_slice(
        jnp.zeros((SMALL, D), jnp.float32), grad_taps, (2, quarter * DQ)
    )
    small_terms = small_terms.at[0].set(grad_gain_one).at[1].set(grad_gain_two)
    small_terms = jnp.pad(small_terms.reshape(D, SMALL), ((0, 0), (0, PAD - SMALL)))
    grad_tail = [
        grad_in.reshape(TEAM, ring, rows, 3 * DQ),
        small_terms.astype(jnp.bfloat16).reshape(TEAM, ring, rows, PAD),
        grad_out.reshape(ring, rows, TEAM, DQ).transpose(2, 0, 1, 3),
    ]
    grad_tail = jnp.concatenate(grad_tail, axis=3)
    grad_tail, grad_down = after(grad_tail, grad_down)
    grad_tail = fold(grad_tail, 1, core_flips)
    grad_tail, (normed_back, grad_up) = after(grad_tail, (normed_back, grad_up))
    grad_up = line_sum(grad_up.reshape(TEAM, line * rows, FQ), 1)
    normed_back = merge(*normed_back)
    grad_tail = fold(grad_tail, 1, line_flips[:1])
    grad_tail, (grad_gate, normed_back, feed_out) = after(
        grad_tail, (grad_gate, normed_back, join(*feed_out))
    )
    feed_out = merge(*feed_out)
    grad_tail = fold(grad_tail, 1, line_flips[1:]).reshape(TEAM, rows, 4 * DQ + PAD)
    feed_out = total(feed_out)
    mixed = (middle + keeper * feed_out).astype(jnp.bfloat16)
    normed_back = total(normed_back)
    unit_one_back = normed_back * gain_one
    inputs_back = middle_back + own_scale * (
        unit_one_back - own_unit * jnp.mean(unit_one_back * own_unit, axis=-1, keepdims=True)
    )
    token_grad = inputs_back.astype(jnp.bfloat16)

    split = 3 * DQ + PAD
    grad_last = jnp.concatenate([grad_tail[:, :, :split], grad_gate, grad_up], axis=2)
    grad_last = swap(pick(grad_last, 0))
    small_grad = sum(part[:, 3 * DQ : 3 * DQ + SMALL].astype(jnp.float32) for part in grad_last)
    small_grad = small_grad.reshape(-1)
    grad_out = grad_tail[:, :, split:].transpose(1, 0, 2).astype(jnp.float32).reshape(-1)

    def columns(parts, groups, width):
        ordered = in_order(parts).astype(jnp.float32).reshape(TEAM, rows, groups, width)
        return ordered.transpose(1, 2, 0, 3).reshape(-1)

    grads = [
        columns([part[:, : 3 * DQ] for part in grad_last], 3, DQ),
        grad_out,
        columns([part[:, split:] for part in grad_last], 2, FQ),
        grad_down.astype(jnp.float32).reshape(-1),
        small_grad,
    ]
    seconds, renewed = [], []
    for i, grad in enumerate(grads):
        span = slice(starts[i], starts[i + 1])
        moment = first_decay * first_moment[span] + (1.0 - first_decay) * grad
        second = second_decay * second_moment[span] + (1.0 - second_decay) * grad * grad
        moment_hat = moment / (1.0 - first_decay**STEP)
        second_hat = second / (1.0 - second_decay**STEP)
        decay = weight_decay if i < 4 else 0.0
        step = moment_hat / (jnp.sqrt(second_hat) + moment_epsilon) + decay * share[i]
        seconds.append(second)
        renewed.append(share[i] - learn_rate * step)
    param_grad = jnp.concatenate(grads)
    second_new = jnp.concatenate(seconds)
    params_new = jnp.concatenate(renewed)
    return (mixed, token_grad, param_grad, small_grad, second_new, params_new)


def solution(mesh):
    placed = (
        P(AXES, None),
        P(AXES, None),
        P(),
        P(),
        P(),
        P(AXES),
        P(AXES),
        P(AXES),
    )
    return jax.shard_map(
        local,
        mesh=mesh,
        in_specs=placed,
        out_specs=(P(AXES, None), P(AXES, None), P(AXES), P(AXES), P(AXES), P(AXES)),
        check_vma=False,
    )
```

```python
import jax
import jax.numpy as jnp
from jax import lax
from jax.sharding import PartitionSpec as P

D = 1024
FF = 4608
STEP = 10
AXES = ("rep", "zero")
TEAM = 4
DQ = D // TEAM
FQ = FF // TEAM
SMALL = 5
PAD = 128

norm_epsilon = 1e-05
first_decay = 0.9
second_decay = 0.999
moment_epsilon = 1e-08
weight_decay = 0.1
learn_rate = 0.06


def rms_scale(values):
    return lax.rsqrt(jnp.mean(values * values, axis=-1, keepdims=True) + norm_epsilon)


def shift_down(values, steps):
    return jnp.pad(values, ((steps, 0), (0, 0)))[: values.shape[0]]


def shift_up(values, steps):
    return jnp.pad(values, ((0, steps), (0, 0)))[steps:]


def matmul(left, right):
    return jnp.dot(left, right, preferred_element_type=jnp.float32)


def over_rows(left, right):
    return lax.dot_general(
        left, right, (((0,), (0,)), ((), ())), preferred_element_type=jnp.float32
    )


def against(left, right):
    return lax.dot_general(
        left, right, (((1,), (1,)), ((), ())), preferred_element_type=jnp.float32
    )


def slot_masks(seq_len, seq_dev, seq_off, owners, slots):
    index = jnp.arange(slots, dtype=jnp.int32)[None, :, None]
    mine = seq_dev[None, None, :] == owners[:, None, None]
    start = seq_off[None, None, :]
    covers = mine & (index >= start) & (index < start + seq_len[None, None, :])
    live = jnp.any(covers, axis=-1)
    opening = jnp.sum(jnp.where(covers, start, 0), axis=-1)
    position = index[:, :, 0] - opening
    column = lambda flags: flags.astype(jnp.float32).reshape(-1, 1)
    return column(live), column(live & (position >= 1)), column(live & (position >= 2))


def local(tokens, cotangent, seq_len, seq_dev, seq_off, params, first_moment, second_moment):
    shards = lax.axis_size(AXES)
    line = lax.axis_size("zero")
    device = lax.axis_index(AXES)
    ring = shards // TEAM
    quarter = device >> (ring.bit_length() - 1)
    slots = tokens.shape[0]
    rings = [[q * ring + w for w in range(ring)] for q in range(TEAM)]
    peers = [quarter ^ j for j in range(TEAM)]

    def send(value, flip):
        return lax.ppermute(value, AXES, [(k, k ^ flip) for k in range(shards)])

    def reach(value):
        return value, send(value, ring), send(value, 2 * ring)

    def cross(value, beside, above):
        half = value.shape[0] // 2
        across = [send(above[:half], ring), send(beside[half:], 2 * ring)]
        return [value, beside, above, jnp.concatenate(across, axis=0)]

    def spread(value):
        return cross(*reach(value))

    def shed(blocks):
        half = blocks[3].shape[0] // 2
        return blocks, send(blocks[3][:half], ring), send(blocks[3][half:], 2 * ring)

    def join(blocks, upper, lower):
        half = upper.shape[0]
        wide = [block.astype(jnp.float32) for block in (blocks[1], blocks[2], upper, lower)]
        beside = jnp.concatenate([wide[0][:half], wide[0][half:] + wide[3]], axis=0)
        above = jnp.concatenate([wide[1][:half] + wide[2], wide[1][half:]], axis=0)
        return blocks[0], beside.astype(jnp.bfloat16), above.astype(jnp.bfloat16)

    def merge(own, beside, above):
        return own, send(beside, ring), send(above, 2 * ring)

    def total(parts):
        return sum(part.astype(jnp.float32) for part in parts)

    def swap(blocks):
        return [blocks[0]] + [send(blocks[j], j * ring) for j in range(1, TEAM)]

    def in_order(pieces):
        odd, high = (quarter & 1) == 1, (quarter >> 1) == 1
        low = [jnp.where(odd, pieces[i ^ 1], pieces[i]) for i in range(TEAM)]
        return jnp.stack([jnp.where(high, low[i ^ 2], low[i]) for i in range(TEAM)])

    def take(table, index, axis):
        return lax.dynamic_index_in_dim(
            table, index, axis=axis, keepdims=False, allow_negative_indices=False
        )

    def pick(table, axis):
        return [take(table, peer, axis) for peer in peers]

    def after(value, earlier):
        return lax.optimization_barrier((value, earlier))

    def ring_gather(value, axis):
        return lax.all_gather(value, AXES, axis=axis, tiled=True, axis_index_groups=rings)

    core_flips = [ring >> i for i in range(1, ring.bit_length()) if ring >> i >= line]
    line_flips = [1 << i for i in range(line.bit_length() - 1)]

    def line_sum(value, axis):
        return lax.psum_scatter(value, "zero", scatter_dimension=axis, tiled=True)

    def fold(value, axis, flips):
        for flip in flips:
            shape = value.shape
            half = shape[axis] // 2
            cut, place = ((2, half), axis) if flip >= line else ((half, 2), axis + 1)
            value = value.reshape(shape[:axis] + cut + shape[axis + 1 :])
            bit = (device >> (flip.bit_length() - 1)) & 1
            other = send(take(value, 1 - bit, place), flip)
            value = take(value, bit, place).astype(jnp.float32) + other.astype(jnp.float32)
            value = value.astype(jnp.bfloat16)
        return value

    rows = D // shards
    sizes = (rows * 3 * D, rows * D, rows * 2 * FF, FF // shards * D, SMALL * rows)
    starts = [sum(sizes[:i]) for i in range(6)]
    share = [params[starts[i] : starts[i + 1]] for i in range(5)]
    low = [part.astype(jnp.bfloat16) for part in share]

    deep = FF // shards
    block_small = jnp.pad(low[4].reshape(rows, SMALL), ((0, 0), (0, PAD - SMALL)))
    block_in = pick(low[0].reshape(rows, 3, TEAM, DQ), 2)
    block_in = [jnp.concatenate([b.reshape(rows, 3 * DQ), block_small], axis=1) for b in block_in]
    block_in = swap(block_in)
    block_in[1], own_tokens = after(block_in[1], tokens)
    token_parts = spread(own_tokens)
    block_out = low[1].reshape(rows, TEAM, DQ).transpose(1, 0, 2)
    ring_in = ring_gather(jnp.concatenate([in_order(block_in), block_out], axis=2), 1)

    token_parts[1], (token_parts[2], block_gu) = after(token_parts[1], (token_parts[2], low[2]))
    block_gu = pick(block_gu.reshape(rows, 2, TEAM, FQ), 2)
    block_gu = in_order(swap([b.reshape(rows, 2 * FQ) for b in block_gu]))
    weight_gateup = ring_gather(block_gu, 1).reshape(D, 2 * FQ)
    weight_down = ring_gather(low[3].reshape(deep, D), 0)
    weight_out = ring_in[:, :, 3 * DQ + PAD :].transpose(1, 0, 2).reshape(DQ, D)
    weight_out = spread(weight_out)
    weight_in = ring_in[:, :, : 3 * DQ].reshape(D, 3 * DQ)
    small = ring_in[:, :, 3 * DQ : 3 * DQ + SMALL].astype(jnp.float32).reshape(SMALL, D)
    gain_one = small[0]
    gain_two = small[1]
    taps = lax.dynamic_slice(small, (2, quarter * DQ), (3, DQ))

    owners = jnp.stack([device ^ (j * ring) for j in range(TEAM)])
    live, reach_one, reach_two = slot_masks(seq_len, seq_dev, seq_off, owners, slots)
    keeper = live[:slots]

    inputs = jnp.concatenate(token_parts, axis=0).astype(jnp.float32)
    unit_one = inputs * rms_scale(inputs)
    normed = (unit_one * gain_one).astype(jnp.bfloat16)
    mixin = matmul(normed, weight_in)
    b_part = mixin[:, :DQ]
    c_part = mixin[:, DQ : 2 * DQ]
    v_part = mixin[:, 2 * DQ :]
    product = b_part * v_part
    lag_one = shift_down(product, 1) * reach_one
    lag_two = shift_down(product, 2) * reach_two
    convolved = taps[0] * product + taps[1] * lag_one + taps[2] * lag_two
    gated = (c_part * convolved).astype(jnp.bfloat16)
    gated = swap([gated[j * slots : (j + 1) * slots] for j in range(TEAM)])

    own = tokens.astype(jnp.float32)
    own_scale = rms_scale(own)
    own_unit = own * own_scale
    branch = sum(matmul(gated[j], weight_out[j]) for j in range(TEAM))
    middle = own + keeper * branch
    scale_two = rms_scale(middle)
    unit_two = middle * scale_two
    normed_two = (unit_two * gain_two).astype(jnp.bfloat16)
    normed_two = spread(normed_two)
    normed_two, late_cotangent = after(normed_two, cotangent)
    normed_two = jnp.concatenate(normed_two, axis=0)
    cotangent_parts = reach(late_cotangent)
    gate_up = matmul(normed_two, weight_gateup)
    gate_up, cotangent_parts = after(gate_up, cotangent_parts)
    upstream = jnp.concatenate(cross(*cotangent_parts), axis=0).astype(jnp.float32)
    feed_back = (live * upstream).astype(jnp.bfloat16)
    gate_part = gate_up[:, :FQ]
    up_part = gate_up[:, FQ:]
    sigma = jax.nn.sigmoid(gate_part)
    swish = gate_part * sigma
    hidden = (swish * up_part).astype(jnp.bfloat16)
    hidden_back = against(feed_back, weight_down)
    gate_back = hidden_back * up_part * (sigma + gate_part * sigma * (1.0 - sigma))
    up_back = hidden_back * swish
    gateup_back = jnp.concatenate([gate_back, up_back], axis=1).astype(jnp.bfloat16)

    spans = [slice(j * slots, (j + 1) * slots) for j in range(TEAM)]
    normed_two_back = against(gateup_back, weight_gateup).astype(jnp.bfloat16)
    normed_two_back = [normed_two_back[span] for span in spans]
    normed_two_back, hidden = after(normed_two_back, hidden)
    grad_down = over_rows(hidden, feed_back).astype(jnp.bfloat16)
    grad_down = fold(grad_down.reshape(ring, deep, D), 0, core_flips)
    normed_two_back, normed_two = after(join(*shed(normed_two_back)), normed_two)
    normed_two_back = merge(*normed_two_back)
    grad_gate = over_rows(normed_two, gateup_back[:, :FQ]).astype(jnp.bfloat16)
    grad_gate = fold(grad_gate.reshape(TEAM, ring, rows, FQ), 1, core_flips)
    normed_two_back, grad_down = after(normed_two_back, grad_down)
    grad_down = line_sum(grad_down.reshape(line * deep, D), 0)
    normed_two_back = total(normed_two_back)

    grad_gain_two = jnp.sum(normed_two_back * unit_two, axis=0)
    unit_two_back = normed_two_back * gain_two
    own_back = cotangent.astype(jnp.float32)
    middle_back = own_back + scale_two * (
        unit_two_back - unit_two * jnp.mean(unit_two_back * unit_two, axis=-1, keepdims=True)
    )
    branch_back = (keeper * middle_back).astype(jnp.bfloat16)
    gated_back = [against(branch_back, weight_out[j]).astype(jnp.bfloat16) for j in range(TEAM)]
    gated_back, (gated, branch_back) = after(gated_back, (gated, branch_back))
    gated_back = swap(gated_back)
    grad_out = shed([over_rows(gated[j], branch_back).astype(jnp.bfloat16) for j in range(TEAM)])
    gated_back, grad_gate = after(gated_back, grad_gate)
    grad_gate = line_sum(grad_gate.reshape(TEAM, line * rows, FQ), 1)
    gated_back = jnp.concatenate(gated_back, axis=0).astype(jnp.float32)

    conv_back = gated_back * c_part
    c_back = gated_back * convolved
    grad_taps = jnp.stack(
        [
            jnp.sum(conv_back * product, axis=0),
            jnp.sum(conv_back * lag_one, axis=0),
            jnp.sum(conv_back * lag_two, axis=0),
        ]
    )
    grad_taps, grad_out = after(grad_taps, grad_out)
    grad_out = merge(*join(*grad_out))
    product_back = (
        taps[0] * conv_back
        + shift_up(taps[1] * conv_back * reach_one, 1)
        + shift_up(taps[2] * conv_back * reach_two, 2)
    )
    mixin_back = jnp.concatenate(
        [product_back * v_part, c_back, product_back * b_part], axis=1
    ).astype(jnp.bfloat16)
    mixin_back, normed_two = after(mixin_back, normed_two)
    grad_up = over_rows(normed_two, gateup_back[:, FQ:]).astype(jnp.bfloat16)
    grad_up = fold(grad_up.reshape(TEAM, ring, rows, FQ), 1, core_flips)
    grad_in = over_rows(normed, mixin_back).astype(jnp.bfloat16)
    grad_in, (hidden, grad_down) = after(grad_in, (hidden, grad_down))
    feed_out = matmul(hidden, weight_down).astype(jnp.bfloat16)
    normed_back = against(mixin_back, weight_in)
    grad_gain_one = jnp.sum(normed_back * unit_one, axis=0)
    normed_back = normed_back.astype(jnp.bfloat16)
    normed_back = [normed_back[span] for span in spans]
    grad_out = total(grad_out).astype(jnp.bfloat16)
    normed_back, feed_out = after(join(*shed(normed_back)), feed_out)
    feed_out = shed([feed_out[span] for span in spans])

    small_terms = lax.dynamic_update_slice(
        jnp.zeros((SMALL, D), jnp.float32), grad_taps, (2, quarter * DQ)
    )
    small_terms = small_terms.at[0].set(grad_gain_one).at[1].set(grad_gain_two)
    small_terms = jnp.pad(small_terms.reshape(D, SMALL), ((0, 0), (0, PAD - SMALL)))
    grad_tail = [
        grad_in.reshape(TEAM, ring, rows, 3 * DQ),
        small_terms.astype(jnp.bfloat16).reshape(TEAM, ring, rows, PAD),
        grad_out.reshape(ring, rows, TEAM, DQ).transpose(2, 0, 1, 3),
    ]
    grad_tail = jnp.concatenate(grad_tail, axis=3)
    grad_tail = fold(grad_tail, 1, core_flips)
    grad_tail, (normed_back, grad_up) = after(grad_tail, (normed_back, grad_up))
    grad_up = line_sum(grad_up.reshape(TEAM, line * rows, FQ), 1)
    normed_back = merge(*normed_back)
    grad_tail = fold(grad_tail, 1, line_flips[:1])
    grad_tail, (grad_gate, normed_back, feed_out) = after(
        grad_tail, (grad_gate, normed_back, join(*feed_out))
    )
    feed_out = merge(*feed_out)
    grad_tail = fold(grad_tail, 1, line_flips[1:]).reshape(TEAM, rows, 4 * DQ + PAD)
    feed_out = total(feed_out)
    mixed = (middle + keeper * feed_out).astype(jnp.bfloat16)
    normed_back = total(normed_back)
    unit_one_back = normed_back * gain_one
    inputs_back = middle_back + own_scale * (
        unit_one_back - own_unit * jnp.mean(unit_one_back * own_unit, axis=-1, keepdims=True)
    )
    token_grad = inputs_back.astype(jnp.bfloat16)

    split = 3 * DQ + PAD
    grad_out = grad_tail[:, :, split:].transpose(1, 0, 2).astype(jnp.float32).reshape(-1)
    grad_last = jnp.concatenate([grad_tail[:, :, :split], grad_gate, grad_up], axis=2)
    grad_last = swap(pick(grad_last, 0))
    small_grad = sum(part[:, 3 * DQ : 3 * DQ + SMALL].astype(jnp.float32) for part in grad_last)
    small_grad = small_grad.reshape(-1)

    def columns(parts, groups, width):
        ordered = in_order(parts).astype(jnp.float32).reshape(TEAM, rows, groups, width)
        return ordered.transpose(1, 2, 0, 3).reshape(-1)

    param_grad = jnp.concatenate(
        [
            columns([part[:, : 3 * DQ] for part in grad_last], 3, DQ),
            grad_out,
            columns([part[:, split:] for part in grad_last], 2, FQ),
            grad_down.astype(jnp.float32).reshape(-1),
            small_grad,
        ]
    )
    shard_len = params.shape[0]
    matrix_mask = (jnp.arange(shard_len) < starts[4]).astype(jnp.float32)
    moment = first_decay * first_moment + (1.0 - first_decay) * param_grad
    second_new = second_decay * second_moment + (1.0 - second_decay) * param_grad * param_grad
    moment_hat = moment / (1.0 - first_decay**STEP)
    second_hat = second_new / (1.0 - second_decay**STEP)
    params_new = params - learn_rate * (
        moment_hat / (jnp.sqrt(second_hat) + moment_epsilon) + weight_decay * matrix_mask * params
    )
    return (mixed, token_grad, param_grad, small_grad, second_new, params_new)


def solution(mesh):
    placed = (
        P(AXES, None),
        P(AXES, None),
        P(),
        P(),
        P(),
        P(AXES),
        P(AXES),
        P(AXES),
    )
    return jax.shard_map(
        local,
        mesh=mesh,
        in_specs=placed,
        out_specs=(P(AXES, None), P(AXES, None), P(AXES), P(AXES), P(AXES), P(AXES)),
        check_vma=False,
    )
```

```python
import jax
import jax.numpy as jnp
from jax import lax
from jax.sharding import PartitionSpec as P

D = 1024
FF = 4608
STEP = 10
AXES = ("rep", "zero")
TEAM = 4
DQ = D // TEAM
FQ = FF // TEAM
SMALL = 5
PAD = 128

norm_epsilon = 1e-05
first_decay = 0.9
second_decay = 0.999
moment_epsilon = 1e-08
weight_decay = 0.1
learn_rate = 0.06


def rms_scale(values):
    return lax.rsqrt(jnp.mean(values * values, axis=-1, keepdims=True) + norm_epsilon)


def shift_down(values, steps):
    return jnp.pad(values, ((steps, 0), (0, 0)))[: values.shape[0]]


def shift_up(values, steps):
    return jnp.pad(values, ((0, steps), (0, 0)))[steps:]


def matmul(left, right):
    return jnp.dot(left, right, preferred_element_type=jnp.float32)


def over_rows(left, right):
    return lax.dot_general(
        left, right, (((0,), (0,)), ((), ())), preferred_element_type=jnp.float32
    )


def against(left, right):
    return lax.dot_general(
        left, right, (((1,), (1,)), ((), ())), preferred_element_type=jnp.float32
    )


def slot_masks(seq_len, seq_dev, seq_off, owners, slots):
    index = jnp.arange(slots, dtype=jnp.int32)[None, :, None]
    mine = seq_dev[None, None, :] == owners[:, None, None]
    start = seq_off[None, None, :]
    covers = mine & (index >= start) & (index < start + seq_len[None, None, :])
    live = jnp.any(covers, axis=-1)
    opening = jnp.sum(jnp.where(covers, start, 0), axis=-1)
    position = index[:, :, 0] - opening
    column = lambda flags: flags.astype(jnp.float32).reshape(-1, 1)
    return column(live), column(live & (position >= 1)), column(live & (position >= 2))


def local(tokens, cotangent, seq_len, seq_dev, seq_off, params, first_moment, second_moment):
    shards = lax.axis_size(AXES)
    line = lax.axis_size("zero")
    device = lax.axis_index(AXES)
    ring = shards // TEAM
    quarter = device >> (ring.bit_length() - 1)
    slots = tokens.shape[0]
    rings = [[q * ring + w for w in range(ring)] for q in range(TEAM)]
    peers = [quarter ^ j for j in range(TEAM)]

    def send(value, flip):
        return lax.ppermute(value, AXES, [(k, k ^ flip) for k in range(shards)])

    def reach(value):
        return value, send(value, ring), send(value, 2 * ring)

    def cross(value, beside, above):
        half = value.shape[0] // 2
        across = [send(above[:half], ring), send(beside[half:], 2 * ring)]
        return [value, beside, above, jnp.concatenate(across, axis=0)]

    def spread(value):
        return cross(*reach(value))

    def shed(blocks):
        half = blocks[3].shape[0] // 2
        return blocks, send(blocks[3][:half], ring), send(blocks[3][half:], 2 * ring)

    def join(blocks, upper, lower):
        half = upper.shape[0]
        wide = [block.astype(jnp.float32) for block in (blocks[1], blocks[2], upper, lower)]
        beside = jnp.concatenate([wide[0][:half], wide[0][half:] + wide[3]], axis=0)
        above = jnp.concatenate([wide[1][:half] + wide[2], wide[1][half:]], axis=0)
        return blocks[0], beside.astype(jnp.bfloat16), above.astype(jnp.bfloat16)

    def merge(own, beside, above):
        return own, send(beside, ring), send(above, 2 * ring)

    def total(parts):
        return sum(part.astype(jnp.float32) for part in parts)

    def swap(blocks):
        return [blocks[0]] + [send(blocks[j], j * ring) for j in range(1, TEAM)]

    def in_order(pieces):
        odd, high = (quarter & 1) == 1, (quarter >> 1) == 1
        low = [jnp.where(odd, pieces[i ^ 1], pieces[i]) for i in range(TEAM)]
        return jnp.stack([jnp.where(high, low[i ^ 2], low[i]) for i in range(TEAM)])

    def take(table, index, axis):
        return lax.dynamic_index_in_dim(
            table, index, axis=axis, keepdims=False, allow_negative_indices=False
        )

    def pick(table, axis):
        return [take(table, peer, axis) for peer in peers]

    def after(value, earlier):
        return lax.optimization_barrier((value, earlier))

    def ring_gather(value, axis):
        return lax.all_gather(value, AXES, axis=axis, tiled=True, axis_index_groups=rings)

    core_flips = [ring >> i for i in range(1, ring.bit_length()) if ring >> i >= line]
    line_flips = [1 << i for i in range(line.bit_length() - 1)]

    def line_sum(value, axis):
        return lax.psum_scatter(value, "zero", scatter_dimension=axis, tiled=True)

    def fold(value, axis, flips):
        for flip in flips:
            shape = value.shape
            half = shape[axis] // 2
            cut, place = ((2, half), axis) if flip >= line else ((half, 2), axis + 1)
            value = value.reshape(shape[:axis] + cut + shape[axis + 1 :])
            bit = (device >> (flip.bit_length() - 1)) & 1
            other = send(take(value, 1 - bit, place), flip)
            value = take(value, bit, place).astype(jnp.float32) + other.astype(jnp.float32)
            value = value.astype(jnp.bfloat16)
        return value

    rows = D // shards
    sizes = (rows * 3 * D, rows * D, rows * 2 * FF, FF // shards * D, SMALL * rows)
    starts = [sum(sizes[:i]) for i in range(6)]
    share = [params[starts[i] : starts[i + 1]] for i in range(5)]
    low = [part.astype(jnp.bfloat16) for part in share]

    deep = FF // shards
    block_small = jnp.pad(low[4].reshape(rows, SMALL), ((0, 0), (0, PAD - SMALL)))
    block_in = pick(low[0].reshape(rows, 3, TEAM, DQ), 2)
    block_in = [jnp.concatenate([b.reshape(rows, 3 * DQ), block_small], axis=1) for b in block_in]
    block_in = swap(block_in)
    block_in[1], own_tokens = after(block_in[1], tokens)
    token_parts = spread(own_tokens)
    block_out = low[1].reshape(rows, TEAM, DQ).transpose(1, 0, 2)
    ring_in = ring_gather(jnp.concatenate([in_order(block_in), block_out], axis=2), 1)

    token_parts[1], (token_parts[2], block_gu) = after(token_parts[1], (token_parts[2], low[2]))
    block_gu = pick(block_gu.reshape(rows, 2, TEAM, FQ), 2)
    block_gu = in_order(swap([b.reshape(rows, 2 * FQ) for b in block_gu]))
    weight_gateup = ring_gather(block_gu, 1).reshape(D, 2 * FQ)
    weight_down = ring_gather(low[3].reshape(deep, D), 0)
    weight_out = ring_in[:, :, 3 * DQ + PAD :].transpose(1, 0, 2).reshape(DQ, D)
    weight_out = spread(weight_out)
    weight_in = ring_in[:, :, : 3 * DQ].reshape(D, 3 * DQ)
    small = ring_in[:, :, 3 * DQ : 3 * DQ + SMALL].astype(jnp.float32).reshape(SMALL, D)
    gain_one = small[0]
    gain_two = small[1]
    taps = lax.dynamic_slice(small, (2, quarter * DQ), (3, DQ))

    owners = jnp.stack([device ^ (j * ring) for j in range(TEAM)])
    live, reach_one, reach_two = slot_masks(seq_len, seq_dev, seq_off, owners, slots)
    keeper = live[:slots]

    inputs = jnp.concatenate(token_parts, axis=0).astype(jnp.float32)
    unit_one = inputs * rms_scale(inputs)
    normed = (unit_one * gain_one).astype(jnp.bfloat16)
    mixin = matmul(normed, weight_in)
    b_part = mixin[:, :DQ]
    c_part = mixin[:, DQ : 2 * DQ]
    v_part = mixin[:, 2 * DQ :]
    product = b_part * v_part
    lag_one = shift_down(product, 1) * reach_one
    lag_two = shift_down(product, 2) * reach_two
    convolved = taps[0] * product + taps[1] * lag_one + taps[2] * lag_two
    gated = (c_part * convolved).astype(jnp.bfloat16)
    gated = swap([gated[j * slots : (j + 1) * slots] for j in range(TEAM)])

    own = tokens.astype(jnp.float32)
    own_scale = rms_scale(own)
    own_unit = own * own_scale
    branch = sum(matmul(gated[j], weight_out[j]) for j in range(TEAM))
    middle = own + keeper * branch
    scale_two = rms_scale(middle)
    unit_two = middle * scale_two
    normed_two = (unit_two * gain_two).astype(jnp.bfloat16)
    normed_two = spread(normed_two)
    normed_two, late_cotangent = after(normed_two, cotangent)
    normed_two = jnp.concatenate(normed_two, axis=0)
    cotangent_parts = reach(late_cotangent)
    gate_up = matmul(normed_two, weight_gateup).astype(jnp.bfloat16)
    gate_up, cotangent_parts = after(gate_up, cotangent_parts)
    upstream = jnp.concatenate(cross(*cotangent_parts), axis=0).astype(jnp.float32)
    feed_back = (live * upstream).astype(jnp.bfloat16)
    gate_part = gate_up[:, :FQ].astype(jnp.float32)
    up_part = gate_up[:, FQ:].astype(jnp.float32)
    sigma = jax.nn.sigmoid(gate_part)
    swish = gate_part * sigma
    hidden = (swish * up_part).astype(jnp.bfloat16)
    hidden_back = against(feed_back, weight_down)
    gate_back = hidden_back * up_part * (sigma + gate_part * sigma * (1.0 - sigma))
    up_back = hidden_back * swish
    gateup_back = jnp.concatenate([gate_back, up_back], axis=1).astype(jnp.bfloat16)

    spans = [slice(j * slots, (j + 1) * slots) for j in range(TEAM)]
    normed_two_back = against(gateup_back, weight_gateup).astype(jnp.bfloat16)
    normed_two_back = [normed_two_back[span] for span in spans]
    normed_two_back, hidden = after(normed_two_back, hidden)
    grad_down = over_rows(hidden, feed_back).astype(jnp.bfloat16)
    grad_down = fold(grad_down.reshape(ring, deep, D), 0, core_flips)
    normed_two_back, normed_two = after(join(*shed(normed_two_back)), normed_two)
    normed_two_back = merge(*normed_two_back)
    grad_gate = over_rows(normed_two, gateup_back[:, :FQ]).astype(jnp.bfloat16)
    grad_gate = fold(grad_gate.reshape(TEAM, ring, rows, FQ), 1, core_flips)
    normed_two_back, grad_down = after(normed_two_back, grad_down)
    grad_down = line_sum(grad_down.reshape(line * deep, D), 0)
    normed_two_back = total(normed_two_back)

    grad_gain_two = jnp.sum(normed_two_back * unit_two, axis=0)
    unit_two_back = normed_two_back * gain_two
    own_back = cotangent.astype(jnp.float32)
    middle_back = own_back + scale_two * (
        unit_two_back - unit_two * jnp.mean(unit_two_back * unit_two, axis=-1, keepdims=True)
    )
    branch_back = (keeper * middle_back).astype(jnp.bfloat16)
    gated_back = [against(branch_back, weight_out[j]).astype(jnp.bfloat16) for j in range(TEAM)]
    gated_back, (gated, branch_back) = after(gated_back, (gated, branch_back))
    gated_back = swap(gated_back)
    grad_out = shed([over_rows(gated[j], branch_back).astype(jnp.bfloat16) for j in range(TEAM)])
    gated_back, grad_gate = after(gated_back, grad_gate)
    grad_gate = line_sum(grad_gate.reshape(TEAM, line * rows, FQ), 1)
    gated_back = jnp.concatenate(gated_back, axis=0).astype(jnp.float32)

    conv_back = gated_back * c_part
    c_back = gated_back * convolved
    grad_taps = jnp.stack(
        [
            jnp.sum(conv_back * product, axis=0),
            jnp.sum(conv_back * lag_one, axis=0),
            jnp.sum(conv_back * lag_two, axis=0),
        ]
    )
    grad_taps, grad_out = after(grad_taps, grad_out)
    grad_out = merge(*join(*grad_out))
    product_back = (
        taps[0] * conv_back
        + shift_up(taps[1] * conv_back * reach_one, 1)
        + shift_up(taps[2] * conv_back * reach_two, 2)
    )
    mixin_back = jnp.concatenate(
        [product_back * v_part, c_back, product_back * b_part], axis=1
    ).astype(jnp.bfloat16)
    mixin_back, normed_two = after(mixin_back, normed_two)
    grad_up = over_rows(normed_two, gateup_back[:, FQ:]).astype(jnp.bfloat16)
    grad_up = fold(grad_up.reshape(TEAM, ring, rows, FQ), 1, core_flips)
    grad_in = over_rows(normed, mixin_back).astype(jnp.bfloat16)
    grad_in, (hidden, grad_down) = after(grad_in, (hidden, grad_down))
    feed_out = matmul(hidden, weight_down).astype(jnp.bfloat16)
    normed_back = against(mixin_back, weight_in)
    grad_gain_one = jnp.sum(normed_back * unit_one, axis=0)
    normed_back = normed_back.astype(jnp.bfloat16)
    normed_back = [normed_back[span] for span in spans]
    grad_out = total(grad_out).astype(jnp.bfloat16)
    normed_back, feed_out = after(join(*shed(normed_back)), feed_out)
    feed_out = shed([feed_out[span] for span in spans])

    small_terms = lax.dynamic_update_slice(
        jnp.zeros((SMALL, D), jnp.float32), grad_taps, (2, quarter * DQ)
    )
    small_terms = small_terms.at[0].set(grad_gain_one).at[1].set(grad_gain_two)
    small_terms = jnp.pad(small_terms.reshape(D, SMALL), ((0, 0), (0, PAD - SMALL)))
    grad_tail = [
        grad_in.reshape(TEAM, ring, rows, 3 * DQ),
        small_terms.astype(jnp.bfloat16).reshape(TEAM, ring, rows, PAD),
        grad_out.reshape(ring, rows, TEAM, DQ).transpose(2, 0, 1, 3),
    ]
    grad_tail = jnp.concatenate(grad_tail, axis=3)
    grad_tail = fold(grad_tail, 1, core_flips)
    grad_tail, (normed_back, grad_up) = after(grad_tail, (normed_back, grad_up))
    grad_up = line_sum(grad_up.reshape(TEAM, line * rows, FQ), 1)
    normed_back = merge(*normed_back)
    grad_tail = fold(grad_tail, 1, line_flips[:1])
    grad_tail, (grad_gate, normed_back, feed_out) = after(
        grad_tail, (grad_gate, normed_back, join(*feed_out))
    )
    feed_out = merge(*feed_out)
    grad_tail = fold(grad_tail, 1, line_flips[1:]).reshape(TEAM, rows, 4 * DQ + PAD)
    feed_out = total(feed_out)
    mixed = (middle + keeper * feed_out).astype(jnp.bfloat16)
    normed_back = total(normed_back)
    unit_one_back = normed_back * gain_one
    inputs_back = middle_back + own_scale * (
        unit_one_back - own_unit * jnp.mean(unit_one_back * own_unit, axis=-1, keepdims=True)
    )
    token_grad = inputs_back.astype(jnp.bfloat16)

    split = 3 * DQ + PAD
    grad_out = grad_tail[:, :, split:].transpose(1, 0, 2).astype(jnp.float32).reshape(-1)
    grad_last = jnp.concatenate([grad_tail[:, :, :split], grad_gate, grad_up], axis=2)
    grad_last = swap(pick(grad_last, 0))
    small_grad = sum(part[:, 3 * DQ : 3 * DQ + SMALL].astype(jnp.float32) for part in grad_last)
    small_grad = small_grad.reshape(-1)

    def columns(parts, groups, width):
        ordered = in_order(parts).astype(jnp.float32).reshape(TEAM, rows, groups, width)
        return ordered.transpose(1, 2, 0, 3).reshape(-1)

    param_grad = jnp.concatenate(
        [
            columns([part[:, : 3 * DQ] for part in grad_last], 3, DQ),
            grad_out,
            columns([part[:, split:] for part in grad_last], 2, FQ),
            grad_down.astype(jnp.float32).reshape(-1),
            small_grad,
        ]
    )
    shard_len = params.shape[0]
    matrix_mask = (jnp.arange(shard_len) < starts[4]).astype(jnp.float32)
    moment = first_decay * first_moment + (1.0 - first_decay) * param_grad
    second_new = second_decay * second_moment + (1.0 - second_decay) * param_grad * param_grad
    moment_hat = moment / (1.0 - first_decay**STEP)
    second_hat = second_new / (1.0 - second_decay**STEP)
    params_new = params - learn_rate * (
        moment_hat / (jnp.sqrt(second_hat) + moment_epsilon) + weight_decay * matrix_mask * params
    )
    return (mixed, token_grad, param_grad, small_grad, second_new, params_new)


def solution(mesh):
    placed = (
        P(AXES, None),
        P(AXES, None),
        P(),
        P(),
        P(),
        P(AXES),
        P(AXES),
        P(AXES),
    )
    return jax.shard_map(
        local,
        mesh=mesh,
        in_specs=placed,
        out_specs=(P(AXES, None), P(AXES, None), P(AXES), P(AXES), P(AXES), P(AXES)),
        check_vma=False,
    )
```
